512 devices in a mesh: row: 16 (over z, core), col: 32 (over y, x).
Axes of the slice: x: 4, y: 8, z: 8, core: 2. Of those that a mesh axis runs over, the one named last changes fastest.
Arguments:
- x_values: bfloat16 [16, 32, 64, 896], P('row', 'col'), may hold values from -0.875 to 0.875
- x_rows: int32 [16, 32, 14], P('row', 'col'), may hold values from -1 to 383, as said below
- x_cols: int32 [16, 32, 14], P('row', 'col'), may hold values from -1 to 383, as said below
- z_rows: int32 [16, 32, 36], P('row', 'col'), may hold values from -1 to 383, as said below
- z_cols: int32 [16, 32, 36], P('row', 'col'), may hold values from -1 to 383, as said below
Outputs:
- y_values: float32 [16, 32, 64, 896], P('row', 'col')
The draws below stay inside these ranges and needn't reach their ends.
Inputs may be any that keep to these rules, and one draw needn't show every extreme that they name: Slot s of the device at (row, col) lists block (x_rows, x_cols); -1 in both marks an unused slot. A listed block row is congruent to the device's row index modulo the size of the row axis, a listed block column to its col index modulo the size of the col axis. No block is listed twice, and each block row and each block column of x holds at most 7 listed blocks. `x_cols`: pairs with x_rows as described there. Slot s of the device at (row, col) lists block (z_rows, z_cols) of the square's pattern; -1 in both marks an unused slot. A listed block row is congruent to the device's row index modulo the size of the row axis, a listed block column to its col index modulo the size of the col axis, and no block is listed twice. `z_cols`: pairs with z_rows as described there.
All inputs are finite; a program needn't handle non-finite values.
Results may differ from the reference program's by a relative error of at most 0.0027.
Values may be sent and summed in bfloat16 or wider, within the bound.
No kernel may reach another device: no remote copies, remote signals or barrier semaphores. Data moves between devices by JAX's collectives and lax.ppermute only.
A program may use at most 128 MiB of HBM per device.

```python
import jax
import jax.numpy as jnp
import numpy as np
from jax import lax

BLK = 64
CELLS_Z = 6
NEIGH = 7
GRID_A = 8
NBLK = 384
XSLOT = 14
ZSLOT = 36
N_ROW = 16
N_COL = 32


def neighbour_steps(twice):
    face_steps = [(0, 0, 0), (1, 0, 0), (-1, 0, 0), (0, 1, 0), (0, -1, 0), (0, 0, 1), (0, 0, -1)]
    if twice:
        combined = sorted({(first_step[0] + second_step[0], first_step[1] + second_step[1], first_step[2] + second_step[2]) for first_step in face_steps for second_step in face_steps})
        return np.array(combined, np.int32)
    return np.array(face_steps, np.int32)


def slot_lists(key, steps, salt, slots):
    relabel = jax.random.permutation(jax.random.fold_in(key, 11), NBLK).astype(jnp.int32)
    cells = jnp.arange(NBLK, dtype=jnp.int32)
    plane = GRID_A * CELLS_Z
    first_axis = cells // plane
    second_axis = cells // CELLS_Z % GRID_A
    third_axis = cells % CELLS_Z
    shifts = jnp.asarray(steps, jnp.int32)
    neighbour = (first_axis[:, None] + shifts[None, :, 0]) % GRID_A * plane
    neighbour = neighbour + (second_axis[:, None] + shifts[None, :, 1]) % GRID_A * CELLS_Z
    neighbour = neighbour + (third_axis[:, None] + shifts[None, :, 2]) % CELLS_Z
    block_row = jnp.broadcast_to(relabel[:, None], neighbour.shape).reshape(-1)
    block_column = relabel[neighbour].reshape(-1)
    number = block_row.shape[0]
    pair_key = block_row * NBLK + block_column
    order = jnp.argsort(pair_key, stable=True)
    sorted_key = pair_key[order]
    repeated = jnp.concatenate([jnp.zeros((1,), bool), sorted_key[1:] == sorted_key[:-1]])
    block_row = block_row[order]
    block_column = block_column[order]
    tiles = N_ROW * N_COL
    tile = jnp.where(repeated, tiles, block_row % N_ROW * N_COL + block_column % N_COL).astype(jnp.int32)
    priority = jax.random.permutation(jax.random.fold_in(key, salt), number).astype(jnp.int32)
    rank_key = tile * number + priority
    second_order = jnp.argsort(rank_key, stable=True)
    tile_sorted = tile[second_order]
    first_position = jnp.searchsorted(tile_sorted, tile_sorted, side='left').astype(jnp.int32)
    rank = jnp.arange(number, dtype=jnp.int32) - first_position
    keep = (tile_sorted < tiles) & (rank < slots)
    target_tile = jnp.where(keep, tile_sorted, tiles)
    target_slot = jnp.where(keep, rank, 0)
    rows_out = jnp.full((tiles + 1, slots), -1, jnp.int32).at[target_tile, target_slot].set(block_row[second_order])
    columns_out = jnp.full((tiles + 1, slots), -1, jnp.int32).at[target_tile, target_slot].set(block_column[second_order])
    rows_out = jnp.where(jnp.arange(tiles + 1)[:, None] < tiles, rows_out, -1)
    return (rows_out[:tiles].reshape(N_ROW, N_COL, slots), columns_out[:tiles].reshape(N_ROW, N_COL, slots))


def draw_x_rows(key, part):
    return slot_lists(key, neighbour_steps(False), 5, XSLOT)[0]


def draw_x_cols(key, part):
    return slot_lists(key, neighbour_steps(False), 5, XSLOT)[1]


def draw_z_rows(key, part):
    return slot_lists(key, neighbour_steps(True), 6, ZSLOT)[0]


def draw_z_cols(key, part):
    return slot_lists(key, neighbour_steps(True), 6, ZSLOT)[1]


def block_levels(stream_key, dims, cuts, smallest, high):
    factor_of = 1.0
    for dim, parts in cuts:
        heights = jax.random.uniform(jax.random.fold_in(jax.random.fold_in(stream_key, 6), dim), (parts,), jnp.float32, smallest / len(cuts), high / len(cuts))
        factor_of = factor_of * jnp.repeat(jnp.exp(heights), dims[dim] // parts).reshape((-1,) + (1,) * (len(dims) - 1 - dim))
    return factor_of


def scatter_about(own_key, shape, spread, most, shards=(), held_as=jnp.bfloat16):
    values = spread * jax.random.normal(own_key, shape, jnp.float32)
    if shards:
        values = values * block_levels(own_key, shape, shards, -0.22, 0.18)
    return jnp.clip(values, -most, most).astype(held_as)


def setup_inputs(seed: int = 0) -> dict:
    streams_of = jax.random.split(jax.random.key(seed), 6)
    return {
        "x_values": scatter_about(streams_of[0], (N_ROW, N_COL, BLK, XSLOT * BLK), (1.2 * BLK ** -0.5), 0.875, ((0, 16), (1, 32))),
        "x_rows": draw_x_rows(jax.random.fold_in(streams_of[5], 71), 0),
        "x_cols": draw_x_cols(jax.random.fold_in(streams_of[5], 71), 0),
        "z_rows": draw_z_rows(jax.random.fold_in(streams_of[5], 71), 0),
        "z_cols": draw_z_cols(jax.random.fold_in(streams_of[5], 71), 0),
    }


def tile_blocks(values, slots):
    tiles = N_ROW * N_COL
    shaped = values.reshape(tiles, BLK, slots, BLK).transpose(0, 2, 1, 3)
    return shaped.reshape(tiles * slots, BLK, BLK)


def slot_table(rows, columns):
    flat_rows = rows.reshape(-1).astype(jnp.int32)
    flat_columns = columns.reshape(-1).astype(jnp.int32)
    listed_count = flat_rows.shape[0]
    place = jnp.where(flat_rows >= 0, flat_rows * NBLK + flat_columns, NBLK * NBLK)
    table = jnp.full((NBLK * NBLK,), listed_count, jnp.int32)
    table = table.at[place].set(jnp.arange(listed_count, dtype=jnp.int32), mode="drop")
    return table.reshape(NBLK, NBLK)


def listed_partners(table, listed_count):
    present = table < listed_count
    score = jnp.where(present, NBLK - jnp.arange(NBLK, dtype=jnp.int32)[None, :], 0).astype(jnp.int32)
    top_values, top_index = lax.top_k(score, NEIGH)
    return jnp.where(top_values > 0, top_index.astype(jnp.int32), -1).astype(jnp.int32)


def reference(x_values, x_rows, x_cols, z_rows, z_cols):
    tiles = N_ROW * N_COL
    x_count = tiles * XSLOT
    z_count = tiles * ZSLOT
    x_blocks = tile_blocks(x_values, XSLOT).astype(jnp.float32)
    x_padded = jnp.concatenate([x_blocks, jnp.zeros((1, BLK, BLK), jnp.float32)], axis=0)
    x_table = slot_table(x_rows, x_cols)
    z_table = slot_table(z_rows, z_cols)
    row_lists = listed_partners(x_table, x_count)
    column_lists = listed_partners(x_table.T, x_count)

    def square_tile(pair):
        rows, columns = pair
        safe_rows = jnp.maximum(rows, 0)
        safe_columns = jnp.maximum(columns, 0)
        partners = row_lists[safe_rows]
        safe_partners = jnp.maximum(partners, 0)
        usable = (rows >= 0)[:, None] & (partners >= 0)
        left = jnp.where(usable, x_table[safe_rows[:, None], safe_partners], x_count)
        right = jnp.where(usable, x_table[safe_partners, safe_columns[:, None]], x_count)
        return jnp.einsum("smik,smkj->sij", x_padded[left], x_padded[right])

    squares = lax.map(square_tile, (z_rows.reshape(tiles, ZSLOT), z_cols.reshape(tiles, ZSLOT)))
    squares = squares.astype(jnp.bfloat16).astype(jnp.float32).reshape(z_count, BLK, BLK)
    z_padded = jnp.concatenate([squares, jnp.zeros((1, BLK, BLK), jnp.float32)], axis=0)

    def cube_tile(pair):
        rows, columns = pair
        safe_rows = jnp.maximum(rows, 0)
        safe_columns = jnp.maximum(columns, 0)
        partners = column_lists[safe_columns]
        safe_partners = jnp.maximum(partners, 0)
        usable = (rows >= 0)[:, None] & (partners >= 0)
        left = jnp.where(usable, z_table[safe_rows[:, None], safe_partners], z_count)
        right = jnp.where(usable, x_table[safe_partners, safe_columns[:, None]], x_count)
        return jnp.einsum("smik,smkj->sij", z_padded[left], x_padded[right])

    cubes = lax.map(cube_tile, (x_rows.reshape(tiles, XSLOT), x_cols.reshape(tiles, XSLOT)))
    own_blocks = x_blocks.reshape(tiles, XSLOT, BLK, BLK)
    used = (x_rows.reshape(tiles, XSLOT) >= 0).astype(jnp.float32)[:, :, None, None]
    result = (1.5 * own_blocks - 0.5 * cubes) * used
    result = result.transpose(0, 2, 1, 3).reshape(N_ROW, N_COL, BLK, XSLOT * BLK)
    return result
```

```python
import functools

import jax
import jax.numpy as jnp
from jax import lax
from jax.experimental import pallas as pl
from jax.experimental.pallas import tpu as pltpu
from jax.sharding import PartitionSpec as P

NEIGH = 7
CORES = 2
NEAR = 4
XROWS = 16
ZROWS = 40
ZSTEP = 64
SEGMENT = NEAR * ZSTEP
FIRST = 12
MORE = 2
META = 16
CODE = 512
LANES = 128
CHUNK = 2
GROUP = 8
STEP = 2
COUNT = 32
FAR = 1e9
PARAMS = pltpu.CompilerParams(vmem_limit_bytes=20 * 1024 * 1024)
VMEM = pl.BlockSpec(memory_space=pltpu.VMEM)
SMEM = pl.BlockSpec(memory_space=pltpu.SMEM)


def lane_numbers(width):
    return lax.broadcasted_iota(jnp.int32, (1, width), 1).astype(jnp.float32)


def following(hits, lanes, last):
    return jnp.min(jnp.where(hits & (lanes > last), lanes, FAR), axis=1, keepdims=True)


def picked(hits, values):
    return jnp.sum(jnp.where(hits, values, 0.0), axis=1, keepdims=True)


def put(table, base, count, good, value):
    return jnp.where((lane_numbers(LANES) == base + count) & good, value, table)


def match_kernel(own_z, own_x, row_x, row_z, col_x, square_list, cube_list):
    row_i, row_m = row_x[0:1, :], row_x[1:2, :]
    col_m, col_k = col_x[0:1, :], col_x[1:2, :]
    row_lanes, col_lanes = lane_numbers(row_i.shape[1]), lane_numbers(col_m.shape[1])
    lane = lane_numbers(LANES)

    i, k = own_z[0][:, :1], own_z[1][:, :1]
    in_row, in_col = (row_i == i) & (i >= 0), (col_k == k) & (k >= 0)
    table = jnp.zeros((ZROWS, LANES), jnp.float32)
    count = jnp.zeros((ZROWS, 1), jnp.float32)
    last = count - 1
    for _ in range(NEIGH):
        last = following(in_row, row_lanes, last)
        middle = picked(row_lanes == last, row_m)
        found = picked(in_col & (col_m == middle), col_lanes + 1)
        good = (last < FAR) & (found > 0)
        table = put(table, 0, count, good, last)
        table = put(table, 8, count, good, found - 1)
        count = count + jnp.where(good, 1.0, 0.0)
    square_list[...] = jnp.where(lane == COUNT, count, table).astype(jnp.int32)

    z_lanes = lane_numbers(row_z.shape[1])
    z_i, z_k = row_z[0:1, :], row_z[1:2, :]
    i, j = own_x[0][:, :1], own_x[1][:, :1]
    in_col = (col_k == j) & (j >= 0)
    needed = jnp.zeros((1, row_z.shape[1]), jnp.float32)
    entries = []
    last = jnp.full((XROWS, 1), -1.0, jnp.float32)
    for _ in range(NEIGH):
        last = following(in_col, col_lanes, last)
        middle = picked(col_lanes == last, col_m)
        hits = (z_i == i) & (z_k == middle) & (last < FAR)
        needed = jnp.maximum(
            needed, jnp.max(jnp.where(hits, 1.0, 0.0), axis=0, keepdims=True)
        )
        entries.append((last, picked(hits, z_lanes + 1) - 1))
    needed = jnp.concatenate(
        [needed[:, n : n + SEGMENT] for n in range(0, needed.shape[1], SEGMENT)], axis=0
    )
    before = (
        lax.broadcasted_iota(jnp.int32, (SEGMENT, SEGMENT), 0)
        < lax.broadcasted_iota(jnp.int32, (SEGMENT, SEGMENT), 1)
    ).astype(jnp.float32)
    rank = jnp.dot(needed, before, preferred_element_type=jnp.float32)
    rank = jnp.concatenate([rank[n : n + 1] for n in range(rank.shape[0])], axis=1)
    table = jnp.zeros((XROWS, LANES), jnp.float32)
    count = jnp.zeros((XROWS, 1), jnp.float32)
    for last, entry in entries:
        good = entry >= 0
        place = picked(z_lanes == entry, rank)
        group = jnp.floor(entry / SEGMENT)
        value = (group * SEGMENT + place) * SEGMENT + entry - group * SEGMENT
        table = put(table, 0, count, good, value)
        table = put(table, 8, count, good, last)
        count = count + jnp.where(good, 1.0, 0.0)
    cube_list[...] = jnp.where(lane == COUNT, count, table).astype(jnp.int32)


def send_kernel(near_z, row_x, cross_x, send_list, loads):
    row_i, row_m = row_x[0:1, :], row_x[1:2, :]
    row_lanes, lane = lane_numbers(row_i.shape[1]), lane_numbers(LANES)
    needs, numbers = [], []
    for n in range(NEAR):
        here = slice(n * ZROWS, (n + 1) * ZROWS)
        i, k = near_z[0][here, :1], near_z[1][here, :1]
        cross_k, cross_j, cross_y = (cross_x[n][t : t + 1, :] for t in range(3))
        in_row, in_cross = (row_i == i) & (i >= 0), (cross_k == k) & (k >= 0)
        need = jnp.zeros((ZROWS, LANES), jnp.float32)
        last = jnp.full((ZROWS, 1), -1.0, jnp.float32)
        for _ in range(NEIGH):
            last = following(in_cross, row_lanes, last)
            target = picked(row_lanes == last, cross_j)
            far = picked(row_lanes == last, cross_y)
            found = picked(in_row & (row_m == target), 1.0)
            need = jnp.where((lane == far) & (last < FAR) & (found > 0), 1.0, need)
        needs.append(need)
        numbers.append(lax.broadcasted_iota(jnp.int32, need.shape, 0) + n * ZSTEP)
    need = jnp.concatenate(needs, axis=0)
    number = jnp.concatenate(numbers, axis=0).astype(jnp.float32)
    size = need.shape[0]
    before = (
        lax.broadcasted_iota(jnp.int32, (size, size), 1)
        < lax.broadcasted_iota(jnp.int32, (size, size), 0)
    ).astype(jnp.float32)
    rank = jnp.dot(before, need, preferred_element_type=jnp.float32)
    rank = jnp.where(need > 0, rank, -1.0)

    def list_rank(p, carry):
        at = rank == p.astype(jnp.float32)
        row = jnp.sum(jnp.where(at, number, 0.0), axis=0, keepdims=True)
        send_list[pl.ds(p, 1), :] = row.astype(jnp.int32)
        return carry

    lax.fori_loop(0, size, list_rank, 0)
    loads[...] = jnp.sum(need, axis=0, keepdims=True).astype(jnp.int32)


def half_mask(half, good):
    lane = lax.broadcasted_iota(jnp.int32, (1, LANES), 1)
    return jnp.where((lane >> 6 == half) & (good > 0), 1.0, 0.0).astype(jnp.bfloat16)


def flat(value):
    return jnp.full((1, LANES), value.astype(jnp.float32)).astype(jnp.bfloat16)


def to_half(tile, half, want):
    swapped = jnp.concatenate([tile[:, 64:], tile[:, :64]], axis=1)
    other = (half != want).astype(jnp.int32)
    return tile * flat(1 - other) + swapped * flat(other)


def pair_up(even, odd):
    even, odd = (tile + pltpu.roll(tile, 64, 1) for tile in (even, odd))
    lane = lax.broadcasted_iota(jnp.int32, even.shape, 1)
    return jnp.where(lane < 64, even, odd)


def add_products(lists, rows, load_left, load_right, sums, chunks):
    sums[...] = jnp.zeros_like(sums)

    def per_row(n, length):
        def one(t, length):
            chunks[length] = (n << 3) + t * CHUNK
            return length + 1

        return lax.fori_loop(0, lax.div(lists[n, COUNT] + CHUNK - 1, CHUNK), one, length)

    length = lax.fori_loop(0, rows - 1, per_row, 0)
    for spare in range(GROUP):
        chunks[length + spare] = (rows - 1) << 3

    def per_group(group, carry):
        values = []
        for n in range(GROUP):
            code = chunks[group * GROUP + n]
            row, start = code >> 3, code & 7
            left, right = [], []
            for t in range(CHUNK):
                place = jnp.minimum(start + t, NEIGH - 1)
                good = (start + t < lists[row, COUNT]).astype(jnp.int32)
                left.append(load_left(lists[row, place], good))
                tile = load_right(lists[row, 8 + place])
                right += [tile, tile]
            left, right = jnp.concatenate(left, axis=1), jnp.concatenate(right, axis=0)
            values.append((row, jnp.dot(left, right, preferred_element_type=jnp.float32)))
        for row, value in values:
            sums[row] += value
        return carry

    lax.fori_loop(0, lax.div(length + GROUP - 1, GROUP), per_group, 0)


def tile_of(entry, step):
    shift = step.bit_length() - 1
    return entry >> shift, (entry & (step - 1)) >> 1, entry & 1


def rows_of(ref, tile):
    return ref.at[pl.ds(pl.multiple_of(tile * 64, 64), 64), :]


def x_tile(ref, entry):
    device, tile, half = tile_of(entry, XROWS)
    return rows_of(ref.at[device], tile)[...] * half_mask(half, 1)


def square_kernel(lists, row_tiles, col_tiles, out_ref, sums, chunks):
    def load_left(entry, good):
        device, tile, half = tile_of(entry, XROWS)
        return row_tiles[device, tile] * half_mask(half, good)

    add_products(
        lists, ZROWS, load_left, functools.partial(x_tile, col_tiles), sums, chunks
    )

    def store(n, carry):
        square = pair_up(sums[2 * n], sums[2 * n + 1]).astype(jnp.bfloat16)
        for copy in range(out_ref.shape[0]):
            out_ref[copy, n] = square
        return carry

    lax.fori_loop(0, out_ref.shape[1], store, 0, unroll=2)


def pack_kernel(info, loads, lists, near, out_ref):
    out_ref[...] = jnp.zeros_like(out_ref)
    first, own = info[0], info[1]
    places = (out_ref.shape[1] - META) // 32
    most = jnp.int32(0)
    for target in range(out_ref.shape[0]):
        most = jnp.maximum(most, jnp.where(own == target, 0, loads[0, target]))

    def per_target(target, carry):
        out_ref[target, places * 32 :, :] = jnp.broadcast_to(flat(most), (META, LANES))
        number = jnp.where(target == own, 0, loads[0, target]) - first
        number = jnp.clip(number, 0, places)

        def per_step(step, carry):
            packed = []
            for n in range(STEP):
                both = []
                for half in range(2):
                    place = step * (2 * STEP) + 2 * n + half
                    good = (place < number).astype(jnp.int32)
                    entry = lists[jnp.minimum(first + place, lists.shape[0] - 1), target]
                    device, tile, side = tile_of(entry, ZSTEP)
                    both.append(to_half(near[device, tile], side, half) * half_mask(half, good))
                packed.append(both[0] + both[1])
            for n, tile in enumerate(packed):
                rows_of(out_ref.at[target], step * STEP + n)[...] = tile
            return carry

        return lax.fori_loop(0, lax.div(number + 2 * STEP - 1, 2 * STEP), per_step, carry)

    lax.fori_loop(0, out_ref.shape[0], per_target, 0)


def cube_kernel(info, lists, near, far, col_tiles, base, out_ref, most_ref, sums, chunks):
    first, own = info[0], info[1]
    places = (far.shape[1] - META) // 32
    most = far[0, places * 32 :, :]
    for n in range(1, far.shape[0]):
        most = jnp.maximum(most, far[n, places * 32 :, :])
    most_ref[0] = jnp.max(most.astype(jnp.float32)).astype(jnp.int32)

    def load_left(code, good):
        group, rank, entry = code >> 16, (code >> 8) & 255, code & 255
        here = group == own
        close = good * (here & (first == 0)).astype(jnp.int32)
        place = rank - first
        inside = (place >= 0) & (place < places) & ~here
        away = good * inside.astype(jnp.int32)
        place = jnp.clip(place, 0, places - 1)
        device, tile, half = tile_of(entry, ZSTEP)
        left = near[device, tile] * half_mask(half, close)
        return left + rows_of(far.at[group], place >> 1)[...] * half_mask(place & 1, away)

    add_products(
        lists, XROWS, load_left, functools.partial(x_tile, col_tiles), sums, chunks
    )
    for n in range(out_ref.shape[1] // LANES):
        here = slice(n * LANES, (n + 1) * LANES)
        out_ref[:, here] = base[:, here] - 0.5 * pair_up(sums[2 * n], sums[2 * n + 1])


def call(kernel, scalars, arrays, out, scratch=()):
    single = isinstance(out, jax.ShapeDtypeStruct)
    return pl.pallas_call(
        kernel,
        out_shape=out,
        in_specs=[SMEM] * len(scalars) + [VMEM] * len(arrays),
        out_specs=VMEM if single else [SMEM if o.shape == (1,) else VMEM for o in out],
        scratch_shapes=scratch,
        compiler_params=PARAMS,
    )(*scalars, *arrays)


def sums_scratch(rows):
    return [
        pltpu.VMEM((rows, 64, LANES), jnp.float32),
        pltpu.SMEM((rows * 4 + 2 * GROUP,), jnp.int32),
    ]


def decode(codes):
    rows = jnp.where(codes >= 0, codes // CODE, -1)
    cols = jnp.where(codes >= 0, codes % CODE, -1)
    return jnp.stack([rows, cols]).astype(jnp.float32)


def encode(rows, cols, length):
    codes = jnp.where(rows >= 0, rows * CODE + cols, -1)
    return jnp.pad(codes, (0, length - codes.shape[0]), constant_values=-1)


def sublanes(pairs):
    return jnp.broadcast_to(pairs[:, :, None], (*pairs.shape, LANES))


def send_all(array, axis, count, **groups):
    copies = jnp.broadcast_to(array, (count, *array.shape))
    return lax.all_to_all(copies, axis, split_axis=0, concat_axis=0, **groups)


def per_device(x_values, x_rows, x_cols, z_rows, z_cols):
    x_rows, x_cols, z_rows, z_cols = (a[0, 0] for a in (x_rows, x_cols, z_rows, z_cols))
    own = x_values[0, 0]
    size, width = own.shape
    n_row, n_col = lax.axis_size("row"), lax.axis_size("col")
    n_far = n_col // NEAR
    col = lax.axis_index("col")
    far_own, near_own = col // NEAR, col % NEAR
    near_groups = [[y * NEAR + x for x in range(NEAR)] for y in range(n_far)]
    far_groups = [[y * NEAR + x for y in range(n_far)] for x in range(NEAR)]
    core_groups = [[z + core for z in range(0, n_row, CORES)] for core in range(CORES)]

    tiles = own.reshape(size, width // LANES, LANES).transpose(1, 0, 2)
    near_tiles = send_all(tiles, "col", NEAR, axis_index_groups=near_groups)
    row_tiles = lax.all_gather(near_tiles, "col", axis=0, axis_index_groups=far_groups)
    row_tiles = row_tiles.reshape(n_col, *tiles.shape)

    x_codes, z_codes = encode(x_rows, x_cols, XROWS), encode(z_rows, z_cols, ZROWS)
    codes = jnp.concatenate([x_codes, z_codes])
    codes = jnp.pad(codes, (0, LANES - codes.shape[0]), constant_values=-1)
    codes, near_tiles = lax.optimization_barrier((codes, near_tiles))
    codes = send_all(codes[None], "col", n_col)[:, 0]
    row_x, row_z = codes[:, :XROWS].reshape(-1), codes[:, XROWS : XROWS + ZROWS]

    meta = jnp.stack([row_x // CODE // n_row, row_x % CODE // n_col])
    meta = jnp.where(row_x >= 0, meta, -1).astype(tiles.dtype).reshape(-1, LANES)
    meta = jnp.pad(meta, ((0, META - meta.shape[0]), (0, 0)))
    labelled = jnp.concatenate([tiles.reshape(-1, LANES), meta])
    col_tiles = send_all(labelled, "row", n_row // CORES, axis_index_groups=core_groups)
    other = lax.ppermute(col_tiles, "row", [(n, n ^ 1) for n in range(n_row)])
    core = lax.axis_index("row") % CORES
    col_tiles = jnp.concatenate([col_tiles, other])
    n_codes = n_col * XROWS
    all_x = col_tiles[:, -META : -META + 2 * n_codes // LANES].astype(jnp.float32)
    all_x = all_x.reshape(CORES, n_row // CORES, 2, n_col, XROWS)
    device = jnp.arange(n_row // CORES) * CORES
    device = jnp.stack([device + core, device + 1 - core]).astype(jnp.float32)

    col_x = lax.dynamic_index_in_dim(all_x, col, 3, keepdims=False)
    col_x = jnp.stack(
        [col_x[:, :, 0] * n_row + device[:, :, None], col_x[:, :, 1] * n_col + col]
    )
    own_places = lax.dynamic_index_in_dim(all_x, col, 3, keepdims=False)[:, :, 0]
    col_x = jnp.where(own_places >= 0, col_x, -1.0).reshape(2, -1)

    row_z_padded = jnp.pad(row_z, ((0, 0), (0, ZSTEP - ZROWS)), constant_values=-1)

    def table(rows):
        return jax.ShapeDtypeStruct((rows, LANES), jnp.int32)

    row_codes = decode(row_x)
    square_list, cube_list = call(
        match_kernel,
        (),
        (
            sublanes(decode(z_codes)),
            sublanes(decode(x_codes)),
            row_codes,
            decode(row_z_padded.reshape(-1)),
            col_x,
        ),
        (table(ZROWS), table(XROWS)),
    )

    start = far_own * NEAR % n_row // CORES
    cross = lax.dynamic_slice_in_dim(all_x, start, NEAR // CORES, 1)
    rows = lax.dynamic_slice_in_dim(device, start, NEAR // CORES, 1)
    in_order = core == 0
    cross = jnp.where(in_order, cross, cross[::-1]).transpose(1, 0, 2, 3, 4)
    rows = jnp.where(in_order, rows, rows[::-1]).transpose(1, 0).reshape(NEAR, 1, 1)
    cross = cross.reshape(NEAR, 2, n_col, XROWS)
    device = jnp.arange(n_col)[:, None]
    cross_k = cross[:, 0] * n_row + rows
    cross_j = cross[:, 1] * n_col + device.astype(jnp.float32)
    cross_k = jnp.where((cross[:, 0] >= 0) & (device % NEAR == near_own), cross_k, -1.0)
    cross_y = jnp.broadcast_to((device // NEAR).astype(jnp.float32), cross_j.shape)
    cross_x = jnp.stack([cross_k, cross_j, cross_y], axis=1).reshape(NEAR, 3, -1)
    near_z = lax.dynamic_slice_in_dim(row_z, far_own * NEAR, NEAR, 0).reshape(-1)
    send_list, loads = call(
        send_kernel,
        (),
        (sublanes(decode(near_z)), row_codes, cross_x),
        (table(NEAR * ZROWS), table(1)),
    )
    square = call(
        square_kernel,
        (square_list,),
        (row_tiles, col_tiles),
        jax.ShapeDtypeStruct((NEAR, z_rows.shape[0] // 2, size, LANES), jnp.bfloat16),
        sums_scratch(ZROWS),
    )
    near = lax.all_to_all(
        square, "col", split_axis=0, concat_axis=0, axis_index_groups=near_groups
    )

    def one_round(first, base, count):
        info = jnp.stack([first, far_own])
        packed = call(
            pack_kernel,
            (info, loads, send_list),
            (near,),
            jax.ShapeDtypeStruct((n_far, count * size + META, LANES), jnp.bfloat16),
        )
        far = lax.all_to_all(
            packed, "col", split_axis=0, concat_axis=0, axis_index_groups=far_groups
        )
        return call(
            cube_kernel,
            (info, cube_list),
            (near, far, col_tiles, base),
            (
                jax.ShapeDtypeStruct(base.shape, jnp.float32),
                jax.ShapeDtypeStruct((1,), jnp.int32),
            ),
            sums_scratch(XROWS),
        )

    def next_round(state):
        first, base, _ = state
        return (first + 2 * MORE, *one_round(first, base, MORE))

    used = jnp.repeat((x_rows >= 0).astype(jnp.float32), size)
    base = 1.5 * own.astype(jnp.float32) * used[None]
    state = (jnp.int32(2 * FIRST), *one_round(jnp.int32(0), base, FIRST))
    _, result, _ = lax.while_loop(lambda state: state[0] < state[2][0], next_round, state)
    return result[None, None]


def solution(mesh):
    placed = (
        P("row", "col", None, None),
        P("row", "col", None),
        P("row", "col", None),
        P("row", "col", None),
        P("row", "col", None),
    )
    return jax.shard_map(
        per_device,
        mesh=mesh,
        in_specs=placed,
        out_specs=P("row", "col", None, None),
        check_vma=False,
    )
```

```python
import functools

import jax
import jax.numpy as jnp
from jax import lax
from jax.experimental import pallas as pl
from jax.experimental.pallas import tpu as pltpu
from jax.sharding import PartitionSpec as P

NEIGH = 7
CODE = 512
CORES = 2
NEAR = 4
XROWS = 16
ZROWS = 40
ZSTEP = 64
SEGMENT = NEAR * ZSTEP
FIRST = 12
MORE = 2
META = 16
LANES = 128
CHUNK = 2
GROUP = 8
STEP = 2
COUNT = 32
FAR = 1e9
MIB = 1024 * 1024
VMEM = pl.BlockSpec(memory_space=pltpu.VMEM)
SMEM = pl.BlockSpec(memory_space=pltpu.SMEM)


def lane_numbers(width):
    return lax.broadcasted_iota(jnp.int32, (1, width), 1).astype(jnp.float32)


def beside(*refs):
    return (jnp.concatenate([ref[n : n + 1, :] for ref in refs], axis=1) for n in range(2))


def following(hits, lanes, last):
    return jnp.min(jnp.where(hits & (lanes > last), lanes, FAR), axis=1, keepdims=True)


def picked(hits, values):
    return jnp.sum(jnp.where(hits, values, 0.0), axis=1, keepdims=True)


def put(table, base, count, good, value):
    return jnp.where((lane_numbers(LANES) == base + count) & good, value, table)


def square_match(own_z, row_x, own_col, other_col, square_list):
    row_i, row_m = row_x[0:1, :], row_x[1:2, :]
    col_m, col_k = beside(own_col, other_col)
    row_lanes, col_lanes = lane_numbers(row_i.shape[1]), lane_numbers(col_m.shape[1])
    lane = lane_numbers(LANES)

    i, k = own_z[0][:, :1], own_z[1][:, :1]
    in_row, in_col = (row_i == i) & (i >= 0), (col_k == k) & (k >= 0)
    table = jnp.zeros((ZROWS, LANES), jnp.float32)
    count = jnp.zeros((ZROWS, 1), jnp.float32)
    last = count - 1
    for _ in range(NEIGH):
        last = following(in_row, row_lanes, last)
        middle = picked(row_lanes == last, row_m)
        found = picked(in_col & (col_m == middle), col_lanes + 1)
        good = (last < FAR) & (found > 0)
        table = put(table, 0, count, good, last)
        table = put(table, 8, count, good, found - 1)
        count = count + jnp.where(good, 1.0, 0.0)
    square_list[...] = jnp.where(lane == COUNT, count, table).astype(jnp.int32)

def cube_match(here, own_x, row_z, own_col, other_col, near_list, far_list):
    col_m, col_k = beside(own_col, other_col)
    col_lanes, lane = lane_numbers(col_m.shape[1]), lane_numbers(LANES)
    z_lanes = lane_numbers(row_z.shape[1])
    z_i, z_k = row_z[0:1, :], row_z[1:2, :]
    i, j = own_x[0][:, :1], own_x[1][:, :1]
    in_col = (col_k == j) & (j >= 0)
    needed = jnp.zeros((1, row_z.shape[1]), jnp.float32)
    entries = []
    last = jnp.full((XROWS, 1), -1.0, jnp.float32)
    for _ in range(NEIGH):
        last = following(in_col, col_lanes, last)
        middle = picked(col_lanes == last, col_m)
        hits = (z_i == i) & (z_k == middle) & (last < FAR)
        needed = jnp.maximum(
            needed, jnp.max(jnp.where(hits, 1.0, 0.0), axis=0, keepdims=True)
        )
        entries.append((last, picked(hits, z_lanes + 1) - 1))
    needed = jnp.concatenate(
        [needed[:, n : n + SEGMENT] for n in range(0, needed.shape[1], SEGMENT)], axis=0
    )
    before = (
        lax.broadcasted_iota(jnp.int32, (SEGMENT, SEGMENT), 0)
        < lax.broadcasted_iota(jnp.int32, (SEGMENT, SEGMENT), 1)
    ).astype(jnp.float32)
    rank = jnp.dot(needed, before, preferred_element_type=jnp.float32)
    n_groups = rank.shape[0]
    rank = jnp.concatenate([rank[n : n + 1] for n in range(rank.shape[0])], axis=1)
    own = here[0].astype(jnp.float32)
    for near, out_ref in ((True, near_list), (False, far_list)):
        table = jnp.zeros((XROWS, LANES), jnp.float32)
        count = jnp.zeros((XROWS, 1), jnp.float32)
        for last, entry in entries:
            group = jnp.floor(entry / SEGMENT)
            entry_of = entry - group * SEGMENT
            if near:
                good = (entry >= 0) & (group == own)
                value = entry_of
            else:
                good = (entry >= 0) & (group != own)
                value = picked(z_lanes == entry, rank) * n_groups + group
            table = put(table, 0, count, good, value)
            table = put(table, 8, count, good, last)
            count = count + jnp.where(good, 1.0, 0.0)
        out_ref[...] = jnp.where(lane == COUNT, count, table).astype(jnp.int32)


def send_kernel(near_z, row_x, cross_x, send_list, loads, ranked):
    row_i, row_m = row_x[0:1, :], row_x[1:2, :]
    row_lanes, lane = lane_numbers(row_i.shape[1]), lane_numbers(LANES)
    needs, numbers = [], []
    for n in range(NEAR):
        here = slice(n * ZROWS, (n + 1) * ZROWS)
        i, k = near_z[0][here, :1], near_z[1][here, :1]
        cross_k, cross_j, cross_y = (cross_x[n][t : t + 1, :] for t in range(3))
        in_row, in_cross = (row_i == i) & (i >= 0), (cross_k == k) & (k >= 0)
        need = jnp.zeros((ZROWS, LANES), jnp.float32)
        last = jnp.full((ZROWS, 1), -1.0, jnp.float32)
        for _ in range(NEIGH):
            last = following(in_cross, row_lanes, last)
            target = picked(row_lanes == last, cross_j)
            far = picked(row_lanes == last, cross_y)
            found = picked(in_row & (row_m == target), 1.0)
            need = jnp.where((lane == far) & (last < FAR) & (found > 0), 1.0, need)
        needs.append(need)
        numbers.append(lax.broadcasted_iota(jnp.int32, need.shape, 0) + n * ZSTEP)
    need = jnp.concatenate(needs, axis=0)
    number = jnp.concatenate(numbers, axis=0).astype(jnp.float32)
    size = need.shape[0]
    before = (
        lax.broadcasted_iota(jnp.int32, (size, size), 1)
        < lax.broadcasted_iota(jnp.int32, (size, size), 0)
    ).astype(jnp.float32)
    rank = jnp.dot(before, need, preferred_element_type=jnp.float32)
    rank = jnp.where(need > 0, rank, -1.0)

    def list_rank(p, carry):
        at = rank == p.astype(jnp.float32)
        row = jnp.sum(jnp.where(at, number, 0.0), axis=0, keepdims=True)
        ranked[pl.ds(p, 1), :] = row
        return carry

    ranked[...] = jnp.zeros_like(ranked)
    lax.fori_loop(0, size, list_rank, 0)
    send_list[...] = ranked[...].T[: send_list.shape[0], :].astype(jnp.int32)
    loads[...] = jnp.sum(need, axis=0, keepdims=True).astype(jnp.int32)


def half_mask(half, good):
    lane = lax.broadcasted_iota(jnp.int32, (1, LANES), 1)
    return jnp.where((lane >> 6 == half) & (good > 0), 1.0, 0.0).astype(jnp.bfloat16)


def flat(value):
    return jnp.full((1, LANES), value.astype(jnp.float32)).astype(jnp.bfloat16)


def to_half(tile, half, want):
    swapped = jnp.concatenate([tile[:, 64:], tile[:, :64]], axis=1)
    other = (half != want).astype(jnp.int32)
    return tile * flat(1 - other) + swapped * flat(other)


def pair_up(even, odd):
    even, odd = (tile + pltpu.roll(tile, 64, 1) for tile in (even, odd))
    lane = lax.broadcasted_iota(jnp.int32, even.shape, 1)
    return jnp.where(lane < 64, even, odd)


def add_products(lists, rows, load_left, load_right, sums, chunks, wait=None):
    sums[...] = jnp.zeros_like(sums)

    def per_row(n, length):
        def one(t, length):
            chunks[length] = (n << 3) + t * CHUNK
            return length + 1

        return lax.fori_loop(0, lax.div(lists[n, COUNT] + CHUNK - 1, CHUNK), one, length)

    length = lax.fori_loop(0, rows - 1, per_row, 0)
    for spare in range(GROUP):
        chunks[length + spare] = (rows - 1) << 3
    if wait is not None:
        wait()

    def per_group(group, carry):
        values = []
        for n in range(GROUP):
            code = chunks[group * GROUP + n]
            row, start = code >> 3, code & 7
            left, right = [], []
            for t in range(CHUNK):
                place = jnp.minimum(start + t, NEIGH - 1)
                good = (start + t < lists[row, COUNT]).astype(jnp.int32)
                left.append(load_left(lists[row, place], good))
                tile = load_right(lists[row, 8 + place])
                right += [tile, tile]
            left, right = jnp.concatenate(left, axis=1), jnp.concatenate(right, axis=0)
            values.append((row, jnp.dot(left, right, preferred_element_type=jnp.float32)))
        for row, value in values:
            sums[row] += value
        return carry

    lax.fori_loop(0, lax.div(length + GROUP - 1, GROUP), per_group, 0)


def tile_of(entry, step):
    shift = step.bit_length() - 1
    return entry >> shift, (entry & (step - 1)) >> 1, entry & 1


def rows_of(ref, tile):
    return ref.at[pl.ds(pl.multiple_of(tile * 64, 64), 64), :]


def x_tile(own, other, entry):
    device, tile, half = tile_of(entry, XROWS)
    shift = own.shape[0].bit_length() - 1
    core, device = device >> shift, device & (own.shape[0] - 1)
    tiles = (rows_of(ref.at[device], tile)[...] for ref in (own, other))
    own_tile, other_tile = tiles
    return own_tile * half_mask(half, 1 - core) + other_tile * half_mask(half, core)


def square_kernel(
    lists, row_hbm, own_tiles, other_tiles, out_ref, sums, chunks, row_tiles, arrived
):
    fetch = pltpu.make_async_copy(row_hbm, row_tiles, arrived)
    fetch.start()

    def load_left(entry, good):
        device, tile, half = tile_of(entry, XROWS)
        return rows_of(row_tiles.at[device], tile)[...] * half_mask(half, good)

    load_right = functools.partial(x_tile, own_tiles, other_tiles)
    add_products(lists, ZROWS, load_left, load_right, sums, chunks, fetch.wait)

    def store(n, carry):
        square = pair_up(sums[2 * n], sums[2 * n + 1]).astype(jnp.bfloat16)
        for copy in range(out_ref.shape[0]):
            out_ref[copy, n] = square
        return carry

    lax.fori_loop(0, out_ref.shape[1], store, 0, unroll=2)


def pack_kernel(info, loads, lists, near, out_ref):
    out_ref[...] = jnp.zeros_like(out_ref)
    first, own = info[0], info[1]
    places = (out_ref.shape[1] - META) // 32
    most = jnp.int32(0)
    for target in range(out_ref.shape[0]):
        most = jnp.maximum(most, jnp.where(own == target, 0, loads[0, target]))

    def per_target(target, carry):
        out_ref[target, places * 32 :, :] = jnp.broadcast_to(flat(most), (META, LANES))
        number = jnp.where(target == own, 0, loads[0, target]) - first
        number = jnp.clip(number, 0, places)

        def per_step(step, carry):
            packed = []
            for n in range(STEP):
                both = []
                for half in range(2):
                    place = step * (2 * STEP) + 2 * n + half
                    good = (place < number).astype(jnp.int32)
                    entry = lists[target, jnp.minimum(first + place, lists.shape[1] - 1)]
                    device, tile, side = tile_of(entry, ZSTEP)
                    both.append(to_half(near[device, tile], side, half) * half_mask(half, good))
                packed.append(both[0] + both[1])
            for n, tile in enumerate(packed):
                rows_of(out_ref.at[target], step * STEP + n)[...] = tile
            return carry

        return lax.fori_loop(0, lax.div(number + 2 * STEP - 1, 2 * STEP), per_step, carry)

    lax.fori_loop(0, out_ref.shape[0], per_target, 0)


def subtract_cubes(sums, base, out_ref):
    for n in range(out_ref.shape[1] // LANES):
        here = slice(n * LANES, (n + 1) * LANES)
        out_ref[:, here] = base[:, here] - 0.5 * pair_up(sums[2 * n], sums[2 * n + 1])


def near_kernel(lists, near, own_tiles, other_tiles, base, out_ref, sums, chunks):
    def load_left(entry, good):
        device, tile, half = tile_of(entry, ZSTEP)
        return near[device, tile] * half_mask(half, good)

    load_right = functools.partial(x_tile, own_tiles, other_tiles)
    add_products(lists, XROWS, load_left, load_right, sums, chunks)
    subtract_cubes(sums, base, out_ref)


def far_kernel(
    info, lists, far, own_tiles, other_tiles, base, out_ref, most_ref, sums, chunks
):
    first = info[0]
    n_groups = far.shape[0]
    shift = n_groups.bit_length() - 1
    places = (far.shape[1] - META) // 32
    most = far[0, places * 32 :, :]
    for n in range(1, n_groups):
        most = jnp.maximum(most, far[n, places * 32 :, :])
    most_ref[0] = jnp.max(most.astype(jnp.float32)).astype(jnp.int32)

    def load_left(code, good):
        group, place = code & (n_groups - 1), (code >> shift) - first
        good = good * ((place >= 0) & (place < places)).astype(jnp.int32)
        place = jnp.clip(place, 0, places - 1)
        return rows_of(far.at[group], place >> 1)[...] * half_mask(place & 1, good)

    load_right = functools.partial(x_tile, own_tiles, other_tiles)
    add_products(lists, XROWS, load_left, load_right, sums, chunks)
    subtract_cubes(sums, base, out_ref)


def call(kernel, scalars, arrays, out, scratch=(), far_off=0):
    single = isinstance(out, jax.ShapeDtypeStruct)
    return pl.pallas_call(
        kernel,
        out_shape=out,
        in_specs=[SMEM] * len(scalars)
        + [pl.BlockSpec(memory_space=pl.ANY)] * far_off
        + [VMEM] * (len(arrays) - far_off),
        out_specs=VMEM if single else [SMEM if o.shape == (1,) else VMEM for o in out],
        scratch_shapes=scratch,
        compiler_params=pltpu.CompilerParams(vmem_limit_bytes=(58 if far_off else 20) * MIB),
    )(*scalars, *arrays)


def sums_scratch(rows):
    return [
        pltpu.VMEM((rows, 64, LANES), jnp.float32),
        pltpu.SMEM((rows * 4 + 2 * GROUP,), jnp.int32),
    ]


def numbers(found, n_row, row, n_col, col):
    lines = jnp.stack([found[0] * n_row + row, found[1] * n_col + col])
    return jnp.where(found[0] >= 0, lines, -1.0)


def listed(rows, cols, length):
    lines = jnp.stack([rows, cols])
    return jnp.pad(lines, ((0, 0), (0, length - rows.shape[0])), constant_values=-1)


def sublanes(pairs):
    return jnp.broadcast_to(pairs[:, :, None], (*pairs.shape, LANES))


def send_all(array, axis, count, **groups):
    copies = jnp.broadcast_to(array, (count, *array.shape))
    return lax.all_to_all(copies, axis, split_axis=0, concat_axis=0, **groups)


def per_device(x_values, x_rows, x_cols, z_rows, z_cols):
    x_rows, x_cols, z_rows, z_cols = (a[0, 0] for a in (x_rows, x_cols, z_rows, z_cols))
    own = x_values[0, 0]
    size, width = own.shape
    n_row, n_col = lax.axis_size("row"), lax.axis_size("col")
    n_far = n_col // NEAR
    col = lax.axis_index("col")
    far_own, near_own = col // NEAR, col % NEAR
    near_groups = [[y * NEAR + x for x in range(NEAR)] for y in range(n_far)]
    far_groups = [[y * NEAR + x for y in range(n_far)] for x in range(NEAR)]
    core_groups = [[z + core for z in range(0, n_row, CORES)] for core in range(CORES)]

    row = lax.axis_index("row")

    tiles = own.reshape(size, width // LANES, LANES).transpose(1, 0, 2).reshape(-1, LANES)
    near_tiles = send_all(tiles, "col", NEAR, axis_index_groups=near_groups)
    row_tiles = lax.all_gather(near_tiles, "col", axis=0, axis_index_groups=far_groups)
    row_tiles = row_tiles.reshape(n_col, -1, LANES)

    own_x, own_z = listed(x_rows, x_cols, XROWS), listed(z_rows, z_cols, ZROWS)
    codes = jnp.concatenate([own_x, own_z], axis=1)
    codes = jnp.where(codes[0] >= 0, codes[0] * CODE + codes[1], -1)
    codes = jnp.pad(codes, (0, LANES - codes.shape[0]), constant_values=-1)
    codes, near_tiles = lax.optimization_barrier((codes, near_tiles))
    codes = send_all(codes[None], "col", n_col)[:, 0]
    lines = jnp.where(codes >= 0, jnp.stack([codes // CODE, codes % CODE]), -1)
    row_x = lines[:, :, :XROWS].reshape(2, -1).astype(jnp.float32)
    row_z = lines[:, :, XROWS : XROWS + ZROWS].astype(jnp.float32)

    meta = jnp.stack([codes // CODE // n_row, codes % CODE // n_col])
    meta = jnp.where(codes >= 0, meta, -1)[:, :, :XROWS].astype(own.dtype).reshape(-1, LANES)
    meta = jnp.pad(meta, ((0, META - meta.shape[0]), (0, 0)))
    labelled = jnp.concatenate([tiles, meta])
    own_tiles = send_all(labelled, "row", n_row // CORES, axis_index_groups=core_groups)
    other_tiles = lax.ppermute(own_tiles, "row", [(n, n ^ 1) for n in range(n_row)])
    core = row % CORES
    devices = jnp.arange(n_col, dtype=jnp.float32)[:, None]
    rows = jnp.arange(n_row // CORES) * CORES
    rows = jnp.stack([rows + core, rows + 1 - core]).astype(jnp.float32)[:, :, None]
    n_lines = 2 * n_col * XROWS // LANES

    def listed_there(t):
        found = t[:, -META : n_lines - META].astype(jnp.float32)
        return found.reshape(n_row // CORES, 2, n_col, XROWS).transpose(1, 0, 2, 3)

    def in_own_col(found, rows):
        found = lax.dynamic_index_in_dim(found, col, 2, keepdims=False)
        return numbers(found, n_row, rows, n_col, col).reshape(2, -1)

    all_x = [listed_there(t) for t in (own_tiles, other_tiles)]
    col_x = [in_own_col(found, rows[n]) for n, found in enumerate(all_x)]
    all_x = jnp.stack(all_x, axis=1)

    def table(rows):
        return jax.ShapeDtypeStruct((rows, LANES), jnp.int32)

    own_z = sublanes(own_z.astype(jnp.float32))
    square_list = call(square_match, (), (own_z, row_x, *col_x), table(ZROWS))

    start = far_own * NEAR % n_row // CORES
    cross = lax.dynamic_slice_in_dim(all_x, start, NEAR // CORES, 2)
    rows = lax.dynamic_slice_in_dim(rows, start, NEAR // CORES, 1)
    in_order = core == 0
    cross = jnp.where(in_order, cross, cross[:, ::-1]).transpose(0, 2, 1, 3, 4)
    rows = jnp.where(in_order, rows, rows[::-1]).transpose(1, 0, 2).reshape(NEAR, 1, 1)
    cross = cross.reshape(2, NEAR, n_col, XROWS)
    cross = numbers(cross, n_row, rows, n_col, devices)
    targets = jnp.arange(n_col)[:, None]
    cross_k = jnp.where(targets % NEAR == near_own, cross[0], -1.0)
    cross_y = jnp.broadcast_to((targets // NEAR).astype(jnp.float32), cross_k.shape)
    cross_x = jnp.stack([cross_k, cross[1], cross_y], axis=1).reshape(NEAR, 3, -1)
    near_z = lax.dynamic_slice_in_dim(row_z, far_own * NEAR, NEAR, 1).reshape(2, -1)
    row_z = jnp.pad(row_z, ((0, 0), (0, 0), (0, ZSTEP - ZROWS)), constant_values=-1)
    own_x = sublanes(own_x.astype(jnp.float32))
    near_list, far_list = call(
        cube_match,
        (far_own.reshape(1),),
        (own_x, row_z.reshape(2, -1), *col_x),
        (table(XROWS), table(XROWS)),
    )
    send_list, loads = call(
        send_kernel,
        (),
        (sublanes(near_z), row_x, cross_x),
        (jax.ShapeDtypeStruct((n_far, SEGMENT), jnp.int32), table(1)),
        [pltpu.VMEM((SEGMENT, LANES), jnp.float32)],
    )
    square = call(
        square_kernel,
        (square_list,),
        (row_tiles, own_tiles, other_tiles),
        jax.ShapeDtypeStruct((NEAR, z_rows.shape[0] // 2, size, LANES), jnp.bfloat16),
        [
            *sums_scratch(ZROWS),
            pltpu.VMEM(row_tiles.shape, row_tiles.dtype),
            pltpu.SemaphoreType.DMA,
        ],
        far_off=1,
    )
    near = lax.all_to_all(
        square, "col", split_axis=0, concat_axis=0, axis_index_groups=near_groups
    )

    def one_round(first, base, count):
        info = jnp.stack([first, far_own])
        packed = call(
            pack_kernel,
            (info, loads, send_list),
            (near,),
            jax.ShapeDtypeStruct((n_far, count * size + META, LANES), jnp.bfloat16),
        )
        far = lax.all_to_all(
            packed, "col", split_axis=0, concat_axis=0, axis_index_groups=far_groups
        )
        return call(
            far_kernel,
            (info, far_list),
            (far, own_tiles, other_tiles, base),
            (
                jax.ShapeDtypeStruct(base.shape, jnp.float32),
                jax.ShapeDtypeStruct((1,), jnp.int32),
            ),
            sums_scratch(XROWS),
        )

    def next_round(state):
        first, base, _ = state
        return (first + 2 * MORE, *one_round(first, base, MORE))

    used = jnp.repeat((x_rows >= 0).astype(jnp.float32), size)
    base = 1.5 * own.astype(jnp.float32) * used[None]
    base = call(
        near_kernel,
        (near_list,),
        (near, own_tiles, other_tiles, base),
        jax.ShapeDtypeStruct(base.shape, jnp.float32),
        sums_scratch(XROWS),
    )
    state = (jnp.int32(2 * FIRST), *one_round(jnp.int32(0), base, FIRST))
    _, result, _ = lax.while_loop(lambda state: state[0] < state[2][0], next_round, state)
    return result[None, None]


def solution(mesh):
    placed = (
        P("row", "col", None, None),
        P("row", "col", None),
        P("row", "col", None),
        P("row", "col", None),
        P("row", "col", None),
    )
    return jax.shard_map(
        per_device,
        mesh=mesh,
        in_specs=placed,
        out_specs=P("row", "col", None, None),
        check_vma=False,
    )
```

```python
import functools

import jax
import jax.numpy as jnp
from jax import lax
from jax.experimental import pallas as pl
from jax.experimental.pallas import tpu as pltpu
from jax.sharding import PartitionSpec as P

NEIGH = 7
CODE = 512
CORES = 2
NEAR = 4
XROWS = 16
ZROWS = 40
ZSTEP = 64
SEGMENT = NEAR * ZSTEP
FIRST = 12
MORE = 2
META = 16
LANES = 128
CHUNK = 2
GROUP = 8
STEP = 2
COUNT = 32
FAR = 1e9
MIB = 1024 * 1024
VMEM = pl.BlockSpec(memory_space=pltpu.VMEM)
SMEM = pl.BlockSpec(memory_space=pltpu.SMEM)


def lane_numbers(width):
    return lax.broadcasted_iota(jnp.int32, (1, width), 1).astype(jnp.float32)


def upright(row):
    return jnp.broadcast_to(row, (LANES, LANES)).T


def beside(*refs):
    return (jnp.concatenate([ref[n : n + 1, :] for ref in refs], axis=1) for n in range(2))


def following(hits, lanes, last):
    return jnp.min(jnp.where(hits & (lanes > last), lanes, FAR), axis=1, keepdims=True)


def picked(hits, values):
    return jnp.sum(jnp.where(hits, values, 0.0), axis=1, keepdims=True)


def put(table, base, count, good, value):
    return jnp.where((lane_numbers(LANES) == base + count) & good, value, table)


def square_match(own_z, row_x, own_col, other_col):
    row_i, row_m = row_x[0:1, :], row_x[1:2, :]
    col_m, col_k = beside(own_col, other_col)
    row_lanes, col_lanes = lane_numbers(row_i.shape[1]), lane_numbers(col_m.shape[1])
    lane = lane_numbers(LANES)

    i, k = (upright(own_z[n : n + 1, :])[:ZROWS, :1] for n in range(2))
    in_row, in_col = (row_i == i) & (i >= 0), (col_k == k) & (k >= 0)
    table = jnp.zeros((ZROWS, LANES), jnp.float32)
    count = jnp.zeros((ZROWS, 1), jnp.float32)
    last = count - 1
    for _ in range(NEIGH):
        last = following(in_row, row_lanes, last)
        middle = picked(row_lanes == last, row_m)
        found = picked(in_col & (col_m == middle), col_lanes + 1)
        good = (last < FAR) & (found > 0)
        table = put(table, 0, count, good, last)
        table = put(table, 8, count, good, found - 1)
        count = count + jnp.where(good, 1.0, 0.0)
    return jnp.where(lane == COUNT, count, table).astype(jnp.int32)

def cube_match(here, own_x, row_z, own_col, other_col, near_list, far_list):
    col_m, col_k = beside(own_col, other_col)
    col_lanes, lane = lane_numbers(col_m.shape[1]), lane_numbers(LANES)
    z_lanes = lane_numbers(row_z.shape[1])
    z_i, z_k = row_z[0:1, :], row_z[1:2, :]
    i, j = own_x[0][:, :1], own_x[1][:, :1]
    in_col = (col_k == j) & (j >= 0)
    needed = jnp.zeros((1, row_z.shape[1]), jnp.float32)
    entries = []
    last = jnp.full((XROWS, 1), -1.0, jnp.float32)
    for _ in range(NEIGH):
        last = following(in_col, col_lanes, last)
        middle = picked(col_lanes == last, col_m)
        hits = (z_i == i) & (z_k == middle) & (last < FAR)
        needed = jnp.maximum(
            needed, jnp.max(jnp.where(hits, 1.0, 0.0), axis=0, keepdims=True)
        )
        entries.append((last, picked(hits, z_lanes + 1) - 1))
    needed = jnp.concatenate(
        [needed[:, n : n + SEGMENT] for n in range(0, needed.shape[1], SEGMENT)], axis=0
    )
    before = (
        lax.broadcasted_iota(jnp.int32, (SEGMENT, SEGMENT), 0)
        < lax.broadcasted_iota(jnp.int32, (SEGMENT, SEGMENT), 1)
    ).astype(jnp.float32)
    rank = jnp.dot(needed, before, preferred_element_type=jnp.float32)
    n_groups = rank.shape[0]
    rank = jnp.concatenate([rank[n : n + 1] for n in range(rank.shape[0])], axis=1)
    own = here[0].astype(jnp.float32)
    for near, out_ref in ((True, near_list), (False, far_list)):
        table = jnp.zeros((XROWS, LANES), jnp.float32)
        count = jnp.zeros((XROWS, 1), jnp.float32)
        for last, entry in entries:
            group = jnp.floor(entry / SEGMENT)
            entry_of = entry - group * SEGMENT
            if near:
                good = (entry >= 0) & (group == own)
                value = entry_of
            else:
                good = (entry >= 0) & (group != own)
                value = picked(z_lanes == entry, rank) * n_groups + group
            table = put(table, 0, count, good, value)
            table = put(table, 8, count, good, last)
            count = count + jnp.where(good, 1.0, 0.0)
        out_ref[...] = jnp.where(lane == COUNT, count, table).astype(jnp.int32)


def send_kernel(near_z, row_x, cross_x, send_list, loads, ranked):
    row_i, row_m = row_x[0:1, :], row_x[1:2, :]
    row_lanes, lane = lane_numbers(row_i.shape[1]), lane_numbers(LANES)
    needs, numbers = [], []
    for n in range(NEAR):
        here = slice(n * ZROWS, (n + 1) * ZROWS)
        i, k = near_z[0][here, :1], near_z[1][here, :1]
        cross_k, cross_j, cross_y = (cross_x[n][t : t + 1, :] for t in range(3))
        in_row, in_cross = (row_i == i) & (i >= 0), (cross_k == k) & (k >= 0)
        need = jnp.zeros((ZROWS, LANES), jnp.float32)
        last = jnp.full((ZROWS, 1), -1.0, jnp.float32)
        for _ in range(NEIGH):
            last = following(in_cross, row_lanes, last)
            target = picked(row_lanes == last, cross_j)
            far = picked(row_lanes == last, cross_y)
            found = picked(in_row & (row_m == target), 1.0)
            need = jnp.where((lane == far) & (last < FAR) & (found > 0), 1.0, need)
        needs.append(need)
        numbers.append(lax.broadcasted_iota(jnp.int32, need.shape, 0) + n * ZSTEP)
    need = jnp.concatenate(needs, axis=0)
    number = jnp.concatenate(numbers, axis=0).astype(jnp.float32)
    size = need.shape[0]
    before = (
        lax.broadcasted_iota(jnp.int32, (size, size), 1)
        < lax.broadcasted_iota(jnp.int32, (size, size), 0)
    ).astype(jnp.float32)
    rank = jnp.dot(before, need, preferred_element_type=jnp.float32)
    rank = jnp.where(need > 0, rank, -1.0)

    def list_rank(p, carry):
        at = rank == p.astype(jnp.float32)
        row = jnp.sum(jnp.where(at, number, 0.0), axis=0, keepdims=True)
        ranked[pl.ds(p, 1), :] = row
        return carry

    ranked[...] = jnp.zeros_like(ranked)
    lax.fori_loop(0, size, list_rank, 0)
    send_list[...] = ranked[...].T[: send_list.shape[0], :].astype(jnp.int32)
    loads[...] = jnp.sum(need, axis=0, keepdims=True).astype(jnp.int32)


def half_mask(half, good):
    lane = lax.broadcasted_iota(jnp.int32, (1, LANES), 1)
    return jnp.where((lane >> 6 == half) & (good > 0), 1.0, 0.0).astype(jnp.bfloat16)


def flat(value):
    return jnp.full((1, LANES), value.astype(jnp.float32)).astype(jnp.bfloat16)


def to_half(tile, half, want):
    swapped = jnp.concatenate([tile[:, 64:], tile[:, :64]], axis=1)
    other = (half != want).astype(jnp.int32)
    return tile * flat(1 - other) + swapped * flat(other)


def pair_up(even, odd):
    even, odd = (tile + pltpu.roll(tile, 64, 1) for tile in (even, odd))
    lane = lax.broadcasted_iota(jnp.int32, even.shape, 1)
    return jnp.where(lane < 64, even, odd)


def list_chunks(lists, rows, chunks):
    def per_row(n, length):
        def one(t, length):
            chunks[length] = (n << 3) + t * CHUNK
            return length + 1

        return lax.fori_loop(0, lax.div(lists[n, COUNT] + CHUNK - 1, CHUNK), one, length)

    length = lax.fori_loop(0, rows - 1, per_row, 0)
    for spare in range(GROUP):
        chunks[length + spare] = (rows - 1) << 3
    return lax.div(length + GROUP - 1, GROUP)


def add_products(lists, groups, load_left, load_right, sums, chunks):
    sums[...] = jnp.zeros_like(sums)

    def per_group(group, carry):
        values = []
        for n in range(GROUP):
            code = chunks[group * GROUP + n]
            row, start = code >> 3, code & 7
            left, right = [], []
            for t in range(CHUNK):
                place = jnp.minimum(start + t, NEIGH - 1)
                good = (start + t < lists[row, COUNT]).astype(jnp.int32)
                left.append(load_left(lists[row, place], good))
                tile = load_right(row, place)
                right += [tile, tile]
            left, right = jnp.concatenate(left, axis=1), jnp.concatenate(right, axis=0)
            values.append((row, jnp.dot(left, right, preferred_element_type=jnp.float32)))
        for row, value in values:
            sums[row] += value
        return carry

    lax.fori_loop(0, groups, per_group, 0)


def tile_of(entry, step):
    shift = step.bit_length() - 1
    return entry >> shift, (entry & (step - 1)) >> 1, entry & 1


def rows_of(ref, tile):
    return ref.at[pl.ds(pl.multiple_of(tile * 64, 64), 64), :]


def x_tile(lists, own, other, row, place):
    device, tile, half = tile_of(lists[row, 8 + place], XROWS)
    shift = own.shape[0].bit_length() - 1
    core, device = device >> shift, device & (own.shape[0] - 1)
    tiles = (rows_of(ref.at[device], tile)[...] for ref in (own, other))
    own_tile, other_tile = tiles
    return own_tile * half_mask(half, 1 - core) + other_tile * half_mask(half, core)


def square_kernel(
    row_hbm, own_z, row_x, own_col, other_col, own_tiles, other_tiles, out_ref, *scratch
):
    sums, chunks, row_tiles, arrived, table, lists, listed, squares, sent = scratch
    parts = arrived.shape[0]
    step = row_tiles.shape[0] // parts
    fetches = [
        pltpu.make_async_copy(
            row_hbm.at[pl.ds(n * step, step)], row_tiles.at[pl.ds(n * step, step)], arrived.at[n]
        )
        for n in range(parts)
    ]
    for fetch in fetches:
        fetch.start()
    table[...] = square_match(own_z, row_x, own_col, other_col)
    known = pltpu.make_async_copy(table, lists, listed)
    known.start()
    known.wait()
    groups = list_chunks(lists, ZROWS, chunks)
    for fetch in fetches:
        fetch.wait()

    def load_left(entry, good):
        device, tile, half = tile_of(entry, XROWS)
        return rows_of(row_tiles.at[device], tile)[...] * half_mask(half, good)

    load_right = functools.partial(x_tile, lists, own_tiles, other_tiles)
    add_products(lists, groups, load_left, load_right, sums, chunks)

    def store(n, carry):
        square = pair_up(sums[2 * n], sums[2 * n + 1]).astype(jnp.bfloat16)
        for copy in range(out_ref.shape[0]):
            squares[n] = square
        return carry

    lax.fori_loop(0, squares.shape[0], store, 0, unroll=2)
    copies = [
        pltpu.make_async_copy(squares, out_ref.at[n], sent.at[n]) for n in range(out_ref.shape[0])
    ]
    for copy in copies:
        copy.start()
    for copy in copies:
        copy.wait()


def pack_kernel(info, loads, lists, near, sent_ref, out_ref, sent):
    out_ref[...] = jnp.zeros_like(out_ref)
    first, own = info[0], info[1]
    places = (out_ref.shape[1] - META) // 32
    most = jnp.int32(0)
    for target in range(out_ref.shape[0]):
        most = jnp.maximum(most, jnp.where(own == target, 0, loads[0, target]))

    def per_target(target, carry):
        out_ref[target, places * 32 :, :] = jnp.broadcast_to(flat(most), (META, LANES))
        number = jnp.where(target == own, 0, loads[0, target]) - first
        number = jnp.clip(number, 0, places)

        def per_step(step, carry):
            packed = []
            for n in range(STEP):
                both = []
                for half in range(2):
                    place = step * (2 * STEP) + 2 * n + half
                    good = (place < number).astype(jnp.int32)
                    entry = lists[target, jnp.minimum(first + place, lists.shape[1] - 1)]
                    device, tile, side = tile_of(entry, ZSTEP)
                    both.append(to_half(near[device, tile], side, half) * half_mask(half, good))
                packed.append(both[0] + both[1])
            for n, tile in enumerate(packed):
                rows_of(out_ref.at[target], step * STEP + n)[...] = tile
            return carry

        lax.fori_loop(0, lax.div(number + 2 * STEP - 1, 2 * STEP), per_step, 0)
        copy_out(target).start()
        return carry

    def copy_out(target):
        return pltpu.make_async_copy(out_ref.at[target], sent_ref.at[target], sent.at[target])

    def finish(target, carry):
        copy_out(target).wait()
        return carry

    lax.fori_loop(0, out_ref.shape[0], per_target, 0)
    lax.fori_loop(0, out_ref.shape[0], finish, 0)


def subtract_cubes(sums, base, out_ref):
    for n in range(out_ref.shape[1] // LANES):
        here = slice(n * LANES, (n + 1) * LANES)
        out_ref[:, here] = base[:, here] - 0.5 * pair_up(sums[2 * n], sums[2 * n + 1])


def near_kernel(
    lists, far, near, own_tiles, other_tiles, base, out_ref, rights, ahead, sums, chunks
):
    def load_left(entry, good):
        device, tile, half = tile_of(entry, ZSTEP)
        return near[device, tile] * half_mask(half, good)

    load_right = functools.partial(x_tile, lists, own_tiles, other_tiles)
    add_products(lists, list_chunks(lists, XROWS, chunks), load_left, load_right, sums, chunks)
    subtract_cubes(sums, base, out_ref)
    ahead[ahead.shape[0] - 1] = list_chunks(far, XROWS, ahead)

    def ready(row, carry):
        for place in range(NEIGH):
            rights[row, place] = x_tile(far, own_tiles, other_tiles, row, place)
        return carry

    lax.fori_loop(0, XROWS, ready, 0)


def largest(far, most_ref):
    places = (far.shape[1] - META) // 32
    most = far[0, places * 32 :, :]
    for n in range(1, far.shape[0]):
        most = jnp.maximum(most, far[n, places * 32 :, :])
    most_ref[0] = jnp.max(most.astype(jnp.float32)).astype(jnp.int32)


def far_tile(far, first, code, good):
    places = (far.shape[1] - META) // 32
    shift = far.shape[0].bit_length() - 1
    group, place = code & (far.shape[0] - 1), (code >> shift) - first
    good = good * ((place >= 0) & (place < places)).astype(jnp.int32)
    place = jnp.clip(place, 0, places - 1)
    return rows_of(far.at[group], place >> 1)[...] * half_mask(place & 1, good)


def first_kernel(lists, ahead, base_hbm, far, rights, out_ref, most_ref, sums, base, arrived):
    fetch = pltpu.make_async_copy(base_hbm, base, arrived)
    fetch.start()
    largest(far, most_ref)
    groups = ahead[ahead.shape[0] - 1]
    load_left = functools.partial(far_tile, far, 0)
    add_products(lists, groups, load_left, lambda row, place: rights[row, place], sums, ahead)
    fetch.wait()
    subtract_cubes(sums, base, out_ref)


def more_kernel(
    info, lists, far, own_tiles, other_tiles, base, out_ref, most_ref, sums, chunks
):
    largest(far, most_ref)
    load_left = functools.partial(far_tile, far, info[0])
    load_right = functools.partial(x_tile, lists, own_tiles, other_tiles)
    add_products(lists, list_chunks(lists, XROWS, chunks), load_left, load_right, sums, chunks)
    subtract_cubes(sums, base, out_ref)


def call(kernel, scalars, arrays, out, scratch=(), far_off=0, out_spec=VMEM):
    single = isinstance(out, jax.ShapeDtypeStruct)
    return pl.pallas_call(
        kernel,
        out_shape=out,
        in_specs=[SMEM] * len(scalars)
        + [pl.BlockSpec(memory_space=pl.ANY)] * far_off
        + [VMEM] * (len(arrays) - far_off),
        out_specs=out_spec if single else [SMEM if len(o.shape) == 1 else VMEM for o in out],
        scratch_shapes=scratch,
        compiler_params=pltpu.CompilerParams(vmem_limit_bytes=20 * MIB),
    )(*scalars, *arrays)


def sums_scratch(rows):
    return [
        pltpu.VMEM((rows, 64, LANES), jnp.float32),
        pltpu.SMEM((rows * 4 + 2 * GROUP,), jnp.int32),
    ]


def numbers(found, n_row, row, n_col, col):
    lines = jnp.stack([found[0] * n_row + row, found[1] * n_col + col])
    return jnp.where(found[0] >= 0, lines, -1.0)


def listed(rows, cols, length):
    lines = jnp.stack([rows, cols])
    return jnp.pad(lines, ((0, 0), (0, length - rows.shape[0])), constant_values=-1)


def sublanes(pairs):
    return jnp.broadcast_to(pairs[:, :, None], (*pairs.shape, LANES))


def send_all(array, axis, count, **groups):
    copies = jnp.broadcast_to(array, (count, *array.shape))
    return lax.all_to_all(copies, axis, split_axis=0, concat_axis=0, **groups)


def per_device(x_values, x_rows, x_cols, z_rows, z_cols):
    x_rows, x_cols, z_rows, z_cols = (a[0, 0] for a in (x_rows, x_cols, z_rows, z_cols))
    own = x_values[0, 0]
    size, width = own.shape
    n_row, n_col = lax.axis_size("row"), lax.axis_size("col")
    n_far = n_col // NEAR
    col = lax.axis_index("col")
    far_own, near_own = col // NEAR, col % NEAR
    near_groups = [[y * NEAR + x for x in range(NEAR)] for y in range(n_far)]
    far_groups = [[y * NEAR + x for y in range(n_far)] for x in range(NEAR)]
    core_groups = [[z + core for z in range(0, n_row, CORES)] for core in range(CORES)]

    row = lax.axis_index("row")

    tiles = own.reshape(size, width // LANES, LANES).transpose(1, 0, 2).reshape(-1, LANES)
    near_tiles = send_all(tiles, "col", NEAR, axis_index_groups=near_groups)
    row_tiles = lax.all_gather(near_tiles, "col", axis=0, axis_index_groups=far_groups)
    row_tiles = row_tiles.reshape(n_col, -1, LANES)

    own_x, own_z = listed(x_rows, x_cols, XROWS), listed(z_rows, z_cols, ZROWS)
    codes = jnp.concatenate([own_x, own_z], axis=1)
    codes = jnp.where(codes[0] >= 0, codes[0] * CODE + codes[1], -1)
    codes = jnp.pad(codes, (0, LANES - codes.shape[0]), constant_values=-1)
    codes, near_tiles = lax.optimization_barrier((codes, near_tiles))
    codes = send_all(codes[None], "col", n_col)[:, 0]
    lines = jnp.where(codes >= 0, jnp.stack([codes // CODE, codes % CODE]), -1)
    row_x = lines[:, :, :XROWS].reshape(2, -1).astype(jnp.float32)
    row_z = lines[:, :, XROWS : XROWS + ZROWS].astype(jnp.float32)

    meta = jnp.stack([codes // CODE // n_row, codes % CODE // n_col])
    meta = jnp.where(codes >= 0, meta, -1)[:, :, :XROWS].astype(own.dtype).reshape(-1, LANES)
    meta = jnp.pad(meta, ((0, META - meta.shape[0]), (0, 0)))
    labelled = jnp.concatenate([tiles, meta])
    own_tiles = send_all(labelled, "row", n_row // CORES, axis_index_groups=core_groups)
    own_z = jnp.pad(own_z, ((0, 0), (0, LANES - ZROWS)), constant_values=-1).astype(jnp.float32)
    own_tiles, row_x, own_z = lax.optimization_barrier((own_tiles, row_x, own_z))
    other_tiles = lax.ppermute(own_tiles, "row", [(n, n ^ 1) for n in range(n_row)])
    core = row % CORES
    devices = jnp.arange(n_col, dtype=jnp.float32)[:, None]
    rows = jnp.arange(n_row // CORES) * CORES
    rows = jnp.stack([rows + core, rows + 1 - core]).astype(jnp.float32)[:, :, None]
    n_lines = 2 * n_col * XROWS // LANES

    def listed_there(t):
        found = t[:, -META : n_lines - META].astype(jnp.float32)
        return found.reshape(n_row // CORES, 2, n_col, XROWS).transpose(1, 0, 2, 3)

    def in_own_col(found, rows):
        found = lax.dynamic_index_in_dim(found, col, 2, keepdims=False)
        return numbers(found, n_row, rows, n_col, col).reshape(2, -1)

    own_listed = listed_there(own_tiles)
    own_col = in_own_col(own_listed, rows[0])
    other_tiles, own_col = lax.optimization_barrier((other_tiles, own_col))
    other_listed = listed_there(other_tiles)
    col_x = (own_col, in_own_col(other_listed, rows[1]))
    all_x = jnp.stack([own_listed, other_listed], axis=1)

    def table(rows):
        return jax.ShapeDtypeStruct((rows, LANES), jnp.int32)


    start = far_own * NEAR % n_row // CORES
    cross = lax.dynamic_slice_in_dim(all_x, start, NEAR // CORES, 2)
    rows = lax.dynamic_slice_in_dim(rows, start, NEAR // CORES, 1)
    in_order = core == 0
    cross = jnp.where(in_order, cross, cross[:, ::-1]).transpose(0, 2, 1, 3, 4)
    rows = jnp.where(in_order, rows, rows[::-1]).transpose(1, 0, 2).reshape(NEAR, 1, 1)
    cross = cross.reshape(2, NEAR, n_col, XROWS)
    cross = numbers(cross, n_row, rows, n_col, devices)
    targets = jnp.arange(n_col)[:, None]
    cross_k = jnp.where(targets % NEAR == near_own, cross[0], -1.0)
    cross_y = jnp.broadcast_to((targets // NEAR).astype(jnp.float32), cross_k.shape)
    cross_x = jnp.stack([cross_k, cross[1], cross_y], axis=1).reshape(NEAR, 3, -1)
    near_z = lax.dynamic_slice_in_dim(row_z, far_own * NEAR, NEAR, 1).reshape(2, -1)
    row_z = jnp.pad(row_z, ((0, 0), (0, 0), (0, ZSTEP - ZROWS)), constant_values=-1)
    own_x = sublanes(own_x.astype(jnp.float32))
    near_list, far_list = call(
        cube_match,
        (far_own.reshape(1),),
        (own_x, row_z.reshape(2, -1), *col_x),
        (table(XROWS), table(XROWS)),
    )
    send_list, loads = call(
        send_kernel,
        (),
        (sublanes(near_z), row_x, cross_x),
        (jax.ShapeDtypeStruct((n_far, SEGMENT), jnp.int32), table(1)),
        [pltpu.VMEM((SEGMENT, LANES), jnp.float32)],
    )
    square = call(
        square_kernel,
        (),
        (
            pltpu.with_memory_space_constraint(row_tiles, pltpu.HBM),
            own_z,
            row_x,
            *col_x,
            own_tiles,
            other_tiles,
        ),
        jax.ShapeDtypeStruct((NEAR, z_rows.shape[0] // 2, size, LANES), jnp.bfloat16),
        [
            *sums_scratch(ZROWS),
            pltpu.VMEM(row_tiles.shape, row_tiles.dtype),
            pltpu.SemaphoreType.DMA((4,)),
            pltpu.VMEM((ZROWS, LANES), jnp.int32),
            pltpu.SMEM((ZROWS, LANES), jnp.int32),
            pltpu.SemaphoreType.DMA,
            pltpu.VMEM((z_rows.shape[0] // 2, size, LANES), jnp.bfloat16),
            pltpu.SemaphoreType.DMA((NEAR,)),
        ],
        far_off=1,
        out_spec=pl.BlockSpec(memory_space=pl.ANY),
    )
    near = lax.all_to_all(
        square, "col", split_axis=0, concat_axis=0, axis_index_groups=near_groups
    )

    def exchange(first, count):
        info = jnp.stack([first, far_own])
        packed = call(
            pack_kernel,
            (info, loads, send_list),
            (near,),
            jax.ShapeDtypeStruct((n_far, count * size + META, LANES), jnp.bfloat16),
            [
                pltpu.VMEM((n_far, count * size + META, LANES), jnp.bfloat16),
                pltpu.SemaphoreType.DMA((n_far,)),
            ],
            out_spec=pl.BlockSpec(memory_space=pl.ANY),
        )
        far = lax.all_to_all(
            packed, "col", split_axis=0, concat_axis=0, axis_index_groups=far_groups
        )
        return info, far

    used = jnp.repeat((x_rows >= 0).astype(jnp.float32), size)
    base = 1.5 * own.astype(jnp.float32) * used[None]
    ahead = jax.ShapeDtypeStruct((XROWS * 4 + 2 * GROUP,), jnp.int32)
    result, most = jax.ShapeDtypeStruct(base.shape, jnp.float32), jax.ShapeDtypeStruct((1,), jnp.int32)
    rights = pltpu.VMEM((XROWS, NEIGH, size, LANES), own.dtype)
    base, rights, ahead = call(
        near_kernel,
        (near_list, far_list),
        (near, own_tiles, other_tiles, base),
        (result, rights, ahead),
        sums_scratch(XROWS),
    )
    _, far = exchange(jnp.int32(0), FIRST)
    state = call(
        first_kernel,
        (far_list, ahead),
        (pltpu.with_memory_space_constraint(base, pltpu.HBM), far, rights),
        (result, most),
        [
            sums_scratch(XROWS)[0],
            pltpu.VMEM(base.shape, jnp.float32),
            pltpu.SemaphoreType.DMA,
        ],
        far_off=1,
    )

    def more(state):
        first, base, _ = state
        info, far = exchange(first, MORE)
        base, largest_need = call(
            more_kernel,
            (info, far_list),
            (far, own_tiles, other_tiles, base),
            (result, most),
            sums_scratch(XROWS),
        )
        return first + 2 * MORE, base, largest_need

    state = (jnp.int32(2 * FIRST), *state)
    _, result, _ = lax.while_loop(lambda state: state[0] < state[2][0], more, state)
    return result[None, None]


def solution(mesh):
    placed = (
        P("row", "col", None, None),
        P("row", "col", None),
        P("row", "col", None),
        P("row", "col", None),
        P("row", "col", None),
    )
    return jax.shard_map(
        per_device,
        mesh=mesh,
        in_specs=placed,
        out_specs=P("row", "col", None, None),
        check_vma=False,
    )
```

```python
import functools

import jax
import jax.numpy as jnp
from jax import lax
from jax.experimental import pallas as pl
from jax.experimental.pallas import tpu as pltpu
from jax.sharding import PartitionSpec as P

NEIGH = 7
CODE = 512
CORES = 2
NEAR = 4
XROWS = 16
ZROWS = 40
ZSTEP = 64
SEGMENT = NEAR * ZSTEP
FIRST = 12
MORE = 2
META = 16
LANES = 128
CHUNK = 2
GROUP = 16
STEP = 2
COUNT = 32
FAR = 1e9
MIB = 1024 * 1024
VMEM = pl.BlockSpec(memory_space=pltpu.VMEM)
SMEM = pl.BlockSpec(memory_space=pltpu.SMEM)


def lane_numbers(width):
    return lax.broadcasted_iota(jnp.int32, (1, width), 1).astype(jnp.float32)


def upright(row):
    return jnp.broadcast_to(row, (LANES, LANES)).T


def beside(*refs):
    return (jnp.concatenate([ref[n : n + 1, :] for ref in refs], axis=1) for n in range(2))


def following(hits, lanes, last):
    return jnp.min(jnp.where(hits & (lanes > last), lanes, FAR), axis=1, keepdims=True)


def picked(hits, values):
    return jnp.sum(jnp.where(hits, values, 0.0), axis=1, keepdims=True)


def put(table, base, count, good, value):
    return jnp.where((lane_numbers(LANES) == base + count) & good, value, table)


def square_match(own_z, row_x, own_col, other_col):
    row_i, row_m = row_x[0:1, :], row_x[1:2, :]
    col_m, col_k = beside(own_col, other_col)
    row_lanes, col_lanes = lane_numbers(row_i.shape[1]), lane_numbers(col_m.shape[1])
    lane = lane_numbers(LANES)

    i, k = (upright(own_z[n : n + 1, :])[:ZROWS, :1] for n in range(2))
    in_row, in_col = (row_i == i) & (i >= 0), (col_k == k) & (k >= 0)
    table = jnp.zeros((ZROWS, LANES), jnp.float32)
    count = jnp.zeros((ZROWS, 1), jnp.float32)
    last = count - 1
    for _ in range(NEIGH):
        last = following(in_row, row_lanes, last)
        middle = picked(row_lanes == last, row_m)
        found = picked(in_col & (col_m == middle), col_lanes + 1)
        good = (last < FAR) & (found > 0)
        table = put(table, 0, count, good, last)
        table = put(table, 8, count, good, found - 1)
        count = count + jnp.where(good, 1.0, 0.0)
    return jnp.where(lane == COUNT, count, table).astype(jnp.int32)

def cube_match(here, own_x, row_z, own_col, other_col, near_list, far_list):
    col_m, col_k = beside(own_col, other_col)
    col_lanes, lane = lane_numbers(col_m.shape[1]), lane_numbers(LANES)
    z_lanes = lane_numbers(row_z.shape[1])
    z_i, z_k = row_z[0:1, :], row_z[1:2, :]
    i, j = own_x[0][:, :1], own_x[1][:, :1]
    in_col = (col_k == j) & (j >= 0)
    needed = jnp.zeros((1, row_z.shape[1]), jnp.float32)
    entries = []
    last = jnp.full((XROWS, 1), -1.0, jnp.float32)
    for _ in range(NEIGH):
        last = following(in_col, col_lanes, last)
        middle = picked(col_lanes == last, col_m)
        hits = (z_i == i) & (z_k == middle) & (last < FAR)
        needed = jnp.maximum(
            needed, jnp.max(jnp.where(hits, 1.0, 0.0), axis=0, keepdims=True)
        )
        entries.append((last, picked(hits, z_lanes + 1) - 1))
    needed = jnp.concatenate(
        [needed[:, n : n + SEGMENT] for n in range(0, needed.shape[1], SEGMENT)], axis=0
    )
    before = (
        lax.broadcasted_iota(jnp.int32, (SEGMENT, SEGMENT), 0)
        < lax.broadcasted_iota(jnp.int32, (SEGMENT, SEGMENT), 1)
    ).astype(jnp.float32)
    rank = jnp.dot(needed, before, preferred_element_type=jnp.float32)
    n_groups = rank.shape[0]
    rank = jnp.concatenate([rank[n : n + 1] for n in range(rank.shape[0])], axis=1)
    own = here[0].astype(jnp.float32)
    for near, out_ref in ((True, near_list), (False, far_list)):
        table = jnp.zeros((XROWS, LANES), jnp.float32)
        count = jnp.zeros((XROWS, 1), jnp.float32)
        for last, entry in entries:
            group = jnp.floor(entry / SEGMENT)
            entry_of = entry - group * SEGMENT
            if near:
                good = (entry >= 0) & (group == own)
                value = entry_of
            else:
                good = (entry >= 0) & (group != own)
                value = picked(z_lanes == entry, rank) * n_groups + group
            table = put(table, 0, count, good, value)
            table = put(table, 8, count, good, last)
            count = count + jnp.where(good, 1.0, 0.0)
        out_ref[...] = jnp.where(lane == COUNT, count, table).astype(jnp.int32)


def send_kernel(near_z, row_x, cross_x, send_list, loads, ranked):
    row_i, row_m = row_x[0:1, :], row_x[1:2, :]
    row_lanes, lane = lane_numbers(row_i.shape[1]), lane_numbers(LANES)
    needs, numbers = [], []
    for n in range(NEAR):
        here = slice(n * ZROWS, (n + 1) * ZROWS)
        i, k = near_z[0][here, :1], near_z[1][here, :1]
        cross_k, cross_j, cross_y = (cross_x[n][t : t + 1, :] for t in range(3))
        in_row, in_cross = (row_i == i) & (i >= 0), (cross_k == k) & (k >= 0)
        need = jnp.zeros((ZROWS, LANES), jnp.float32)
        last = jnp.full((ZROWS, 1), -1.0, jnp.float32)
        for _ in range(NEIGH):
            last = following(in_cross, row_lanes, last)
            target = picked(row_lanes == last, cross_j)
            far = picked(row_lanes == last, cross_y)
            found = picked(in_row & (row_m == target), 1.0)
            need = jnp.where((lane == far) & (last < FAR) & (found > 0), 1.0, need)
        needs.append(need)
        numbers.append(lax.broadcasted_iota(jnp.int32, need.shape, 0) + n * ZSTEP)
    need = jnp.concatenate(needs, axis=0)
    number = jnp.concatenate(numbers, axis=0).astype(jnp.float32)
    size = need.shape[0]
    before = (
        lax.broadcasted_iota(jnp.int32, (size, size), 1)
        < lax.broadcasted_iota(jnp.int32, (size, size), 0)
    ).astype(jnp.float32)
    rank = jnp.dot(before, need, preferred_element_type=jnp.float32)
    rank = jnp.where(need > 0, rank, -1.0)

    def list_rank(p, carry):
        at = rank == p.astype(jnp.float32)
        row = jnp.sum(jnp.where(at, number, 0.0), axis=0, keepdims=True)
        ranked[pl.ds(p, 1), :] = row
        return carry

    ranked[...] = jnp.zeros_like(ranked)
    lax.fori_loop(0, size, list_rank, 0)
    send_list[...] = ranked[...].T[: send_list.shape[0], :].astype(jnp.int32)
    loads[...] = jnp.sum(need, axis=0, keepdims=True).astype(jnp.int32)


def half_mask(half, good):
    lane = lax.broadcasted_iota(jnp.int32, (1, LANES), 1)
    kept = jnp.where(good > 0, half, 2)
    return jnp.where(lane >> 6 == kept, 1.0, 0.0).astype(jnp.bfloat16)


def flat(value):
    return jnp.full((1, LANES), value.astype(jnp.float32)).astype(jnp.bfloat16)


def to_half(tile, half, want):
    swapped = jnp.concatenate([tile[:, 64:], tile[:, :64]], axis=1)
    other = (half != want).astype(jnp.int32)
    return tile * flat(1 - other) + swapped * flat(other)


def pair_up(even, odd):
    even, odd = (tile + pltpu.roll(tile, 64, 1) for tile in (even, odd))
    lane = lax.broadcasted_iota(jnp.int32, even.shape, 1)
    return jnp.where(lane < 64, even, odd)


def list_chunks(lists, rows, chunks):
    length = jnp.int32(0)
    for n in range(rows - 1):
        for start in range(0, NEIGH, CHUNK):
            chunks[length + start // CHUNK] = (n << 3) + start
        length = length + lax.div(lists[n, COUNT] + CHUNK - 1, CHUNK)
    for spare in range(GROUP):
        chunks[length + spare] = (rows - 1) << 3
    return lax.div(length + GROUP - 1, GROUP)


def add_products(lists, groups, load_left, load_right, sums, chunks):
    sums[...] = jnp.zeros_like(sums)

    def per_group(group, carry):
        values = []
        for n in range(GROUP):
            code = chunks[group * GROUP + n]
            row, start = code >> 3, code & 7
            left, right = [], []
            for t in range(CHUNK):
                place = jnp.minimum(start + t, NEIGH - 1)
                good = (start + t < lists[row, COUNT]).astype(jnp.int32)
                left.append(load_left(lists[row, place], good))
                tile = load_right(row, place)
                right += [tile, tile]
            left, right = jnp.concatenate(left, axis=1), jnp.concatenate(right, axis=0)
            values.append((row, jnp.dot(left, right, preferred_element_type=jnp.float32)))
        for row, value in values:
            sums[row] += value
        return carry

    lax.fori_loop(0, groups, per_group, 0)


def tile_of(entry, step):
    shift = step.bit_length() - 1
    return entry >> shift, (entry & (step - 1)) >> 1, entry & 1


def rows_of(ref, tile):
    return ref.at[pl.ds(pl.multiple_of(tile * 64, 64), 64), :]


def x_tile(lists, own, other, row, place):
    device, tile, half = tile_of(lists[row, 8 + place], XROWS)
    shift = own.shape[0].bit_length() - 1
    core, device = device >> shift, device & (own.shape[0] - 1)
    tiles = (rows_of(ref.at[device], tile)[...] for ref in (own, other))
    own_tile, other_tile = tiles
    return own_tile * half_mask(half, 1 - core) + other_tile * half_mask(half, core)


def square_kernel(
    row_hbm, own_z, row_x, own_col, other_col, own_tiles, other_tiles, out_ref, *scratch
):
    sums, chunks, row_tiles, arrived, table, lists, listed, squares, sent = scratch
    parts = arrived.shape[0]
    step = row_tiles.shape[0] // parts
    fetches = [
        pltpu.make_async_copy(
            row_hbm.at[pl.ds(n * step, step)], row_tiles.at[pl.ds(n * step, step)], arrived.at[n]
        )
        for n in range(parts)
    ]
    for fetch in fetches:
        fetch.start()
    table[...] = square_match(own_z, row_x, own_col, other_col)
    known = pltpu.make_async_copy(table, lists, listed)
    known.start()
    known.wait()
    groups = list_chunks(lists, ZROWS, chunks)
    for fetch in fetches:
        fetch.wait()

    def load_left(entry, good):
        device, tile, half = tile_of(entry, XROWS)
        return rows_of(row_tiles.at[device], tile)[...] * half_mask(half, good)

    load_right = functools.partial(x_tile, lists, own_tiles, other_tiles)
    add_products(lists, groups, load_left, load_right, sums, chunks)

    def store(n, carry):
        square = pair_up(sums[2 * n], sums[2 * n + 1]).astype(jnp.bfloat16)
        for copy in range(out_ref.shape[0]):
            squares[n] = square
        return carry

    lax.fori_loop(0, squares.shape[0], store, 0, unroll=2)
    copies = [
        pltpu.make_async_copy(squares, out_ref.at[n], sent.at[n]) for n in range(out_ref.shape[0])
    ]
    for copy in copies:
        copy.start()
    for copy in copies:
        copy.wait()


def pack_kernel(info, loads, lists, near, sent_ref, out_ref, sent):
    out_ref[...] = jnp.zeros_like(out_ref)
    first, own = info[0], info[1]
    places = (out_ref.shape[1] - META) // 32
    most = jnp.int32(0)
    for target in range(out_ref.shape[0]):
        most = jnp.maximum(most, jnp.where(own == target, 0, loads[0, target]))

    def per_target(target, carry):
        out_ref[target, places * 32 :, :] = jnp.broadcast_to(flat(most), (META, LANES))
        number = jnp.where(target == own, 0, loads[0, target]) - first
        number = jnp.clip(number, 0, places)

        def per_step(step, carry):
            packed = []
            for n in range(STEP):
                both = []
                for half in range(2):
                    place = step * (2 * STEP) + 2 * n + half
                    good = (place < number).astype(jnp.int32)
                    entry = lists[target, jnp.minimum(first + place, lists.shape[1] - 1)]
                    device, tile, side = tile_of(entry, ZSTEP)
                    both.append(to_half(near[device, tile], side, half) * half_mask(half, good))
                packed.append(both[0] + both[1])
            for n, tile in enumerate(packed):
                rows_of(out_ref.at[target], step * STEP + n)[...] = tile
            return carry

        lax.fori_loop(0, lax.div(number + 2 * STEP - 1, 2 * STEP), per_step, 0)
        copy_out(target).start()
        return carry

    def copy_out(target):
        return pltpu.make_async_copy(out_ref.at[target], sent_ref.at[target], sent.at[target])

    def finish(target, carry):
        copy_out(target).wait()
        return carry

    for target in range(out_ref.shape[0]):
        per_target(target, 0)
    lax.fori_loop(0, out_ref.shape[0], finish, 0)


def subtract_cubes(sums, base, out_ref):
    for n in range(out_ref.shape[1] // LANES):
        here = slice(n * LANES, (n + 1) * LANES)
        out_ref[:, here] = base[:, here] - 0.5 * pair_up(sums[2 * n], sums[2 * n + 1])


def near_kernel(
    lists, far, near, own_tiles, other_tiles, base, out_ref, rights, ahead, sums, chunks
):
    def load_left(entry, good):
        device, tile, half = tile_of(entry, ZSTEP)
        return near[device, tile] * half_mask(half, good)

    load_right = functools.partial(x_tile, lists, own_tiles, other_tiles)
    add_products(lists, list_chunks(lists, XROWS, chunks), load_left, load_right, sums, chunks)
    subtract_cubes(sums, base, out_ref)
    ahead[ahead.shape[0] - 1] = list_chunks(far, XROWS, ahead)

    def ready(row, carry):
        for place in range(NEIGH):
            rights[row, place] = x_tile(far, own_tiles, other_tiles, row, place)
        return carry

    lax.fori_loop(0, XROWS, ready, 0)


def largest(far, most_ref):
    places = (far.shape[1] - META) // 32
    most = far[0, places * 32 :, :]
    for n in range(1, far.shape[0]):
        most = jnp.maximum(most, far[n, places * 32 :, :])
    most_ref[0] = jnp.max(most.astype(jnp.float32)).astype(jnp.int32)


def far_tile(far, first, code, good):
    places = (far.shape[1] - META) // 32
    shift = far.shape[0].bit_length() - 1
    group, place = code & (far.shape[0] - 1), (code >> shift) - first
    good = good * ((place >= 0) & (place < places)).astype(jnp.int32)
    place = jnp.clip(place, 0, places - 1)
    return rows_of(far.at[group], place >> 1)[...] * half_mask(place & 1, good)


def first_kernel(lists, ahead, base_hbm, far, rights, out_ref, most_ref, sums, base, arrived):
    fetch = pltpu.make_async_copy(base_hbm, base, arrived)
    fetch.start()
    largest(far, most_ref)
    groups = ahead[ahead.shape[0] - 1]
    load_left = functools.partial(far_tile, far, 0)
    add_products(lists, groups, load_left, lambda row, place: rights[row, place], sums, ahead)
    fetch.wait()
    subtract_cubes(sums, base, out_ref)


def more_kernel(
    info, lists, far, own_tiles, other_tiles, base, out_ref, most_ref, sums, chunks
):
    largest(far, most_ref)
    load_left = functools.partial(far_tile, far, info[0])
    load_right = functools.partial(x_tile, lists, own_tiles, other_tiles)
    add_products(lists, list_chunks(lists, XROWS, chunks), load_left, load_right, sums, chunks)
    subtract_cubes(sums, base, out_ref)


def call(kernel, scalars, arrays, out, scratch=(), far_off=0, out_spec=VMEM):
    single = isinstance(out, jax.ShapeDtypeStruct)
    return pl.pallas_call(
        kernel,
        out_shape=out,
        in_specs=[SMEM] * len(scalars)
        + [pl.BlockSpec(memory_space=pl.ANY)] * far_off
        + [VMEM] * (len(arrays) - far_off),
        out_specs=out_spec if single else [SMEM if len(o.shape) == 1 else VMEM for o in out],
        scratch_shapes=scratch,
        compiler_params=pltpu.CompilerParams(vmem_limit_bytes=20 * MIB),
    )(*scalars, *arrays)


def sums_scratch(rows):
    return [
        pltpu.VMEM((rows, 64, LANES), jnp.float32),
        pltpu.SMEM((rows * 4 + 2 * GROUP,), jnp.int32),
    ]


def numbers(found, n_row, row, n_col, col):
    lines = jnp.stack([found[0] * n_row + row, found[1] * n_col + col])
    return jnp.where(found[0] >= 0, lines, -1.0)


def listed(rows, cols, length):
    lines = jnp.stack([rows, cols])
    return jnp.pad(lines, ((0, 0), (0, length - rows.shape[0])), constant_values=-1)


def sublanes(pairs):
    return jnp.broadcast_to(pairs[:, :, None], (*pairs.shape, LANES))


def send_all(array, axis, count, **groups):
    copies = jnp.broadcast_to(array, (count, *array.shape))
    return lax.all_to_all(copies, axis, split_axis=0, concat_axis=0, **groups)


def per_device(x_values, x_rows, x_cols, z_rows, z_cols):
    x_rows, x_cols, z_rows, z_cols = (a[0, 0] for a in (x_rows, x_cols, z_rows, z_cols))
    own = x_values[0, 0]
    size, width = own.shape
    n_row, n_col = lax.axis_size("row"), lax.axis_size("col")
    n_far = n_col // NEAR
    col = lax.axis_index("col")
    far_own, near_own = col // NEAR, col % NEAR
    near_groups = [[y * NEAR + x for x in range(NEAR)] for y in range(n_far)]
    far_groups = [[y * NEAR + x for y in range(n_far)] for x in range(NEAR)]
    core_groups = [[z + core for z in range(0, n_row, CORES)] for core in range(CORES)]

    row = lax.axis_index("row")

    tiles = own.reshape(size, width // LANES, LANES).transpose(1, 0, 2).reshape(-1, LANES)
    near_tiles = send_all(tiles, "col", NEAR, axis_index_groups=near_groups)
    row_tiles = lax.all_gather(near_tiles, "col", axis=0, axis_index_groups=far_groups)
    row_tiles = row_tiles.reshape(n_col, -1, LANES)

    own_x, own_z = listed(x_rows, x_cols, XROWS), listed(z_rows, z_cols, ZROWS)
    codes = jnp.concatenate([own_x, own_z], axis=1)
    codes = jnp.where(codes[0] >= 0, codes[0] * CODE + codes[1], -1)
    codes = jnp.pad(codes, (0, LANES - codes.shape[0]), constant_values=-1)
    codes, near_tiles = lax.optimization_barrier((codes, near_tiles))
    codes = send_all(codes[None], "col", n_col)[:, 0]
    lines = jnp.where(codes >= 0, jnp.stack([codes // CODE, codes % CODE]), -1)
    row_x = lines[:, :, :XROWS].reshape(2, -1).astype(jnp.float32)
    row_z = lines[:, :, XROWS : XROWS + ZROWS].astype(jnp.float32)

    meta = jnp.stack([codes // CODE // n_row, codes % CODE // n_col])
    meta = jnp.where(codes >= 0, meta, -1)[:, :, :XROWS].astype(own.dtype).reshape(-1, LANES)
    meta = jnp.pad(meta, ((0, META - meta.shape[0]), (0, 0)))
    labelled = jnp.concatenate([tiles, meta])
    own_tiles = send_all(labelled, "row", n_row // CORES, axis_index_groups=core_groups)
    own_z = jnp.pad(own_z, ((0, 0), (0, LANES - ZROWS)), constant_values=-1).astype(jnp.float32)
    own_tiles, row_x, own_z = lax.optimization_barrier((own_tiles, row_x, own_z))
    other_tiles = lax.ppermute(own_tiles, "row", [(n, n ^ 1) for n in range(n_row)])
    core = row % CORES
    devices = jnp.arange(n_col, dtype=jnp.float32)[:, None]
    rows = jnp.arange(n_row // CORES) * CORES
    rows = jnp.stack([rows + core, rows + 1 - core]).astype(jnp.float32)[:, :, None]
    n_lines = 2 * n_col * XROWS // LANES

    def listed_there(t):
        found = t[:, -META : n_lines - META].astype(jnp.float32)
        return found.reshape(n_row // CORES, 2, n_col, XROWS).transpose(1, 0, 2, 3)

    def in_own_col(found, rows):
        found = lax.dynamic_index_in_dim(found, col, 2, keepdims=False)
        return numbers(found, n_row, rows, n_col, col).reshape(2, -1)

    own_listed = listed_there(own_tiles)
    own_col = in_own_col(own_listed, rows[0])
    other_tiles, own_col = lax.optimization_barrier((other_tiles, own_col))
    other_listed = listed_there(other_tiles)
    col_x = (own_col, in_own_col(other_listed, rows[1]))
    all_x = jnp.stack([own_listed, other_listed], axis=1)

    def table(rows):
        return jax.ShapeDtypeStruct((rows, LANES), jnp.int32)


    start = far_own * NEAR % n_row // CORES
    cross = lax.dynamic_slice_in_dim(all_x, start, NEAR // CORES, 2)
    rows = lax.dynamic_slice_in_dim(rows, start, NEAR // CORES, 1)
    in_order = core == 0
    cross = jnp.where(in_order, cross, cross[:, ::-1]).transpose(0, 2, 1, 3, 4)
    rows = jnp.where(in_order, rows, rows[::-1]).transpose(1, 0, 2).reshape(NEAR, 1, 1)
    cross = cross.reshape(2, NEAR, n_col, XROWS)
    cross = numbers(cross, n_row, rows, n_col, devices)
    targets = jnp.arange(n_col)[:, None]
    cross_k = jnp.where(targets % NEAR == near_own, cross[0], -1.0)
    cross_y = jnp.broadcast_to((targets // NEAR).astype(jnp.float32), cross_k.shape)
    cross_x = jnp.stack([cross_k, cross[1], cross_y], axis=1).reshape(NEAR, 3, -1)
    near_z = lax.dynamic_slice_in_dim(row_z, far_own * NEAR, NEAR, 1).reshape(2, -1)
    row_z = jnp.pad(row_z, ((0, 0), (0, 0), (0, ZSTEP - ZROWS)), constant_values=-1)
    own_x = sublanes(own_x.astype(jnp.float32))
    near_list, far_list = call(
        cube_match,
        (far_own.reshape(1),),
        (own_x, row_z.reshape(2, -1), *col_x),
        (table(XROWS), table(XROWS)),
    )
    send_list, loads = call(
        send_kernel,
        (),
        (sublanes(near_z), row_x, cross_x),
        (jax.ShapeDtypeStruct((n_far, SEGMENT), jnp.int32), table(1)),
        [pltpu.VMEM((SEGMENT, LANES), jnp.float32)],
    )
    square = call(
        square_kernel,
        (),
        (
            pltpu.with_memory_space_constraint(row_tiles, pltpu.HBM),
            own_z,
            row_x,
            *col_x,
            own_tiles,
            other_tiles,
        ),
        jax.ShapeDtypeStruct((NEAR, z_rows.shape[0] // 2, size, LANES), jnp.bfloat16),
        [
            *sums_scratch(ZROWS),
            pltpu.VMEM(row_tiles.shape, row_tiles.dtype),
            pltpu.SemaphoreType.DMA((4,)),
            pltpu.VMEM((ZROWS, LANES), jnp.int32),
            pltpu.SMEM((ZROWS, LANES), jnp.int32),
            pltpu.SemaphoreType.DMA,
            pltpu.VMEM((z_rows.shape[0] // 2, size, LANES), jnp.bfloat16),
            pltpu.SemaphoreType.DMA((NEAR,)),
        ],
        far_off=1,
        out_spec=pl.BlockSpec(memory_space=pl.ANY),
    )
    near = lax.all_to_all(
        square, "col", split_axis=0, concat_axis=0, axis_index_groups=near_groups
    )

    def exchange(first, count):
        info = jnp.stack([first, far_own])
        packed = call(
            pack_kernel,
            (info, loads, send_list),
            (near,),
            jax.ShapeDtypeStruct((n_far, count * size + META, LANES), jnp.bfloat16),
            [
                pltpu.VMEM((n_far, count * size + META, LANES), jnp.bfloat16),
                pltpu.SemaphoreType.DMA((n_far,)),
            ],
            out_spec=pl.BlockSpec(memory_space=pl.ANY),
        )
        far = lax.all_to_all(
            packed, "col", split_axis=0, concat_axis=0, axis_index_groups=far_groups
        )
        return info, far

    used = jnp.repeat((x_rows >= 0).astype(jnp.float32), size)
    base = 1.5 * own.astype(jnp.float32) * used[None]
    ahead = jax.ShapeDtypeStruct((XROWS * 4 + 2 * GROUP,), jnp.int32)
    result, most = jax.ShapeDtypeStruct(base.shape, jnp.float32), jax.ShapeDtypeStruct((1,), jnp.int32)
    rights = pltpu.VMEM((XROWS, NEIGH, size, LANES), own.dtype)
    base, rights, ahead = call(
        near_kernel,
        (near_list, far_list),
        (near, own_tiles, other_tiles, base),
        (result, rights, ahead),
        sums_scratch(XROWS),
    )
    _, far = exchange(jnp.int32(0), FIRST)
    state = call(
        first_kernel,
        (far_list, ahead),
        (pltpu.with_memory_space_constraint(base, pltpu.HBM), far, rights),
        (result, most),
        [
            sums_scratch(XROWS)[0],
            pltpu.VMEM(base.shape, jnp.float32),
            pltpu.SemaphoreType.DMA,
        ],
        far_off=1,
    )

    def more(state):
        first, base, _ = state
        info, far = exchange(first, MORE)
        base, largest_need = call(
            more_kernel,
            (info, far_list),
            (far, own_tiles, other_tiles, base),
            (result, most),
            sums_scratch(XROWS),
        )
        return first + 2 * MORE, base, largest_need

    state = (jnp.int32(2 * FIRST), *state)
    _, result, _ = lax.while_loop(lambda state: state[0] < state[2][0], more, state)
    return result[None, None]


def solution(mesh):
    placed = (
        P("row", "col", None, None),
        P("row", "col", None),
        P("row", "col", None),
        P("row", "col", None),
        P("row", "col", None),
    )
    return jax.shard_map(
        per_device,
        mesh=mesh,
        in_specs=placed,
        out_specs=P("row", "col", None, None),
        check_vma=False,
    )
```

```python
import functools

import jax
import jax.numpy as jnp
from jax import lax
from jax.experimental import pallas as pl
from jax.experimental.pallas import tpu as pltpu
from jax.sharding import PartitionSpec as P

NEIGH = 7
CODE = 512
CORES = 2
NEAR = 4
XROWS = 16
ZROWS = 40
ZSTEP = 64
SEGMENT = NEAR * ZSTEP
FIRST = 12
MORE = 2
META = 16
LANES = 128
CHUNK = 2
GROUP = 24
STEP = 2
COUNT = 32
FAR = 1e9
MIB = 1024 * 1024
VMEM = pl.BlockSpec(memory_space=pltpu.VMEM)
SMEM = pl.BlockSpec(memory_space=pltpu.SMEM)


def lane_numbers(width):
    return lax.broadcasted_iota(jnp.int32, (1, width), 1).astype(jnp.float32)


def upright(row):
    return jnp.broadcast_to(row, (LANES, LANES)).T


def beside(*refs):
    return (jnp.concatenate([ref[n : n + 1, :] for ref in refs], axis=1) for n in range(2))


def following(hits, lanes, last):
    return jnp.min(jnp.where(hits & (lanes > last), lanes, FAR), axis=1, keepdims=True)


def picked(hits, values):
    return jnp.sum(jnp.where(hits, values, 0.0), axis=1, keepdims=True)


def put(table, base, count, good, value):
    return jnp.where((lane_numbers(LANES) == base + count) & good, value, table)


def square_match(own_z, row_x, own_col, other_col):
    row_i, row_m = row_x[0:1, :], row_x[1:2, :]
    col_m, col_k = beside(own_col, other_col)
    row_lanes, col_lanes = lane_numbers(row_i.shape[1]), lane_numbers(col_m.shape[1])
    lane = lane_numbers(LANES)

    i, k = (upright(own_z[n : n + 1, :])[:ZROWS, :1] for n in range(2))
    in_row, in_col = (row_i == i) & (i >= 0), (col_k == k) & (k >= 0)
    table = jnp.zeros((ZROWS, LANES), jnp.float32)
    count = jnp.zeros((ZROWS, 1), jnp.float32)
    last = count - 1
    for _ in range(NEIGH):
        last = following(in_row, row_lanes, last)
        middle = picked(row_lanes == last, row_m)
        found = picked(in_col & (col_m == middle), col_lanes + 1)
        good = (last < FAR) & (found > 0)
        table = put(table, 0, count, good, last)
        table = put(table, 8, count, good, found - 1)
        count = count + jnp.where(good, 1.0, 0.0)
    return jnp.where(lane == COUNT, count, table).astype(jnp.int32)

def cube_match(here, own_x, row_z, own_col, other_col, near_list, far_list):
    col_m, col_k = beside(own_col, other_col)
    col_lanes, lane = lane_numbers(col_m.shape[1]), lane_numbers(LANES)
    z_lanes = lane_numbers(row_z.shape[1])
    z_i, z_k = row_z[0:1, :], row_z[1:2, :]
    i, j = own_x[0][:, :1], own_x[1][:, :1]
    in_col = (col_k == j) & (j >= 0)
    needed = jnp.zeros((1, row_z.shape[1]), jnp.float32)
    entries = []
    last = jnp.full((XROWS, 1), -1.0, jnp.float32)
    for _ in range(NEIGH):
        last = following(in_col, col_lanes, last)
        middle = picked(col_lanes == last, col_m)
        hits = (z_i == i) & (z_k == middle) & (last < FAR)
        needed = jnp.maximum(
            needed, jnp.max(jnp.where(hits, 1.0, 0.0), axis=0, keepdims=True)
        )
        entries.append((last, picked(hits, z_lanes + 1) - 1))
    needed = jnp.concatenate(
        [needed[:, n : n + SEGMENT] for n in range(0, needed.shape[1], SEGMENT)], axis=0
    )
    before = (
        lax.broadcasted_iota(jnp.int32, (SEGMENT, SEGMENT), 0)
        < lax.broadcasted_iota(jnp.int32, (SEGMENT, SEGMENT), 1)
    ).astype(jnp.float32)
    rank = jnp.dot(needed, before, preferred_element_type=jnp.float32)
    n_groups = rank.shape[0]
    rank = jnp.concatenate([rank[n : n + 1] for n in range(rank.shape[0])], axis=1)
    own = here[0].astype(jnp.float32)
    for near, out_ref in ((True, near_list), (False, far_list)):
        table = jnp.zeros((XROWS, LANES), jnp.float32)
        count = jnp.zeros((XROWS, 1), jnp.float32)
        for last, entry in entries:
            group = jnp.floor(entry / SEGMENT)
            entry_of = entry - group * SEGMENT
            if near:
                good = (entry >= 0) & (group == own)
                value = entry_of
            else:
                good = (entry >= 0) & (group != own)
                value = picked(z_lanes == entry, rank) * n_groups + group
            table = put(table, 0, count, good, value)
            table = put(table, 8, count, good, last)
            count = count + jnp.where(good, 1.0, 0.0)
        out_ref[...] = jnp.where(lane == COUNT, count, table).astype(jnp.int32)


def send_kernel(near_z, row_x, cross_x, send_list, loads, ranked):
    row_i, row_m = row_x[0:1, :], row_x[1:2, :]
    row_lanes, lane = lane_numbers(row_i.shape[1]), lane_numbers(LANES)
    needs, numbers = [], []
    for n in range(NEAR):
        here = slice(n * ZROWS, (n + 1) * ZROWS)
        i, k = near_z[0][here, :1], near_z[1][here, :1]
        cross_k, cross_j, cross_y = (cross_x[n][t : t + 1, :] for t in range(3))
        in_row, in_cross = (row_i == i) & (i >= 0), (cross_k == k) & (k >= 0)
        need = jnp.zeros((ZROWS, LANES), jnp.float32)
        last = jnp.full((ZROWS, 1), -1.0, jnp.float32)
        for _ in range(NEIGH):
            last = following(in_cross, row_lanes, last)
            target = picked(row_lanes == last, cross_j)
            far = picked(row_lanes == last, cross_y)
            found = picked(in_row & (row_m == target), 1.0)
            need = jnp.where((lane == far) & (last < FAR) & (found > 0), 1.0, need)
        needs.append(need)
        numbers.append(lax.broadcasted_iota(jnp.int32, need.shape, 0) + n * ZSTEP)
    need = jnp.concatenate(needs, axis=0)
    number = jnp.concatenate(numbers, axis=0).astype(jnp.float32)
    size = need.shape[0]
    before = (
        lax.broadcasted_iota(jnp.int32, (size, size), 1)
        < lax.broadcasted_iota(jnp.int32, (size, size), 0)
    ).astype(jnp.float32)
    rank = jnp.dot(before, need, preferred_element_type=jnp.float32)
    rank = jnp.where(need > 0, rank, -1.0)

    def list_rank(p, carry):
        at = rank == p.astype(jnp.float32)
        row = jnp.sum(jnp.where(at, number, 0.0), axis=0, keepdims=True)
        ranked[pl.ds(p, 1), :] = row
        return carry

    ranked[...] = jnp.zeros_like(ranked)
    lax.fori_loop(0, size, list_rank, 0)
    send_list[...] = ranked[...].T[: send_list.shape[0], :].astype(jnp.int32)
    loads[...] = jnp.sum(need, axis=0, keepdims=True).astype(jnp.int32)


def half_mask(half, good):
    lane = lax.broadcasted_iota(jnp.int32, (1, LANES), 1)
    kept = jnp.where(good > 0, half, 2)
    return jnp.where(lane >> 6 == kept, 1.0, 0.0).astype(jnp.bfloat16)


def flat(value):
    return jnp.full((1, LANES), value.astype(jnp.float32)).astype(jnp.bfloat16)


def to_half(tile, half, want):
    swapped = jnp.concatenate([tile[:, 64:], tile[:, :64]], axis=1)
    other = (half != want).astype(jnp.int32)
    return tile * flat(1 - other) + swapped * flat(other)


def pair_up(even, odd):
    even, odd = (tile + pltpu.roll(tile, 64, 1) for tile in (even, odd))
    lane = lax.broadcasted_iota(jnp.int32, even.shape, 1)
    return jnp.where(lane < 64, even, odd)


def list_chunks(lists, rows, chunks):
    length = jnp.int32(0)
    for n in range(rows - 1):
        for start in range(0, NEIGH, CHUNK):
            chunks[length + start // CHUNK] = (n << 3) + start
        length = length + lax.div(lists[n, COUNT] + CHUNK - 1, CHUNK)
    for spare in range(GROUP):
        chunks[length + spare] = (rows - 1) << 3
    return lax.div(length + GROUP - 1, GROUP)


def add_products(lists, groups, load_left, load_right, sums, chunks):
    sums[...] = jnp.zeros_like(sums)

    def per_group(group, carry):
        values = []
        for n in range(GROUP):
            code = chunks[group * GROUP + n]
            row, start = code >> 3, code & 7
            left, right = [], []
            for t in range(CHUNK):
                place = jnp.minimum(start + t, NEIGH - 1)
                good = (start + t < lists[row, COUNT]).astype(jnp.int32)
                left.append(load_left(lists[row, place], good))
                tile = load_right(row, place)
                right += [tile, tile]
            left, right = jnp.concatenate(left, axis=1), jnp.concatenate(right, axis=0)
            values.append((row, jnp.dot(left, right, preferred_element_type=jnp.float32)))
        for row, value in values:
            sums[row] += value
        return carry

    lax.fori_loop(0, groups, per_group, 0)


def tile_of(entry, step):
    shift = step.bit_length() - 1
    return entry >> shift, (entry & (step - 1)) >> 1, entry & 1


def rows_of(ref, tile):
    return ref.at[pl.ds(pl.multiple_of(tile * 64, 64), 64), :]


def x_tile(lists, own, other, row, place):
    device, tile, half = tile_of(lists[row, 8 + place], XROWS)
    shift = own.shape[0].bit_length() - 1
    core, device = device >> shift, device & (own.shape[0] - 1)
    tiles = (rows_of(ref.at[device], tile)[...] for ref in (own, other))
    own_tile, other_tile = tiles
    return own_tile * half_mask(half, 1 - core) + other_tile * half_mask(half, core)


def square_kernel(
    row_hbm, own_z, row_x, own_col, other_col, own_tiles, other_tiles, out_ref, *scratch
):
    sums, chunks, row_tiles, arrived, table, lists, listed, squares, sent = scratch
    parts = arrived.shape[0]
    step = row_tiles.shape[0] // parts
    fetches = [
        pltpu.make_async_copy(
            row_hbm.at[pl.ds(n * step, step)], row_tiles.at[pl.ds(n * step, step)], arrived.at[n]
        )
        for n in range(parts)
    ]
    for fetch in fetches:
        fetch.start()
    table[...] = square_match(own_z, row_x, own_col, other_col)
    known = pltpu.make_async_copy(table, lists, listed)
    known.start()
    known.wait()
    groups = list_chunks(lists, ZROWS, chunks)
    for fetch in fetches:
        fetch.wait()

    def load_left(entry, good):
        device, tile, half = tile_of(entry, XROWS)
        return rows_of(row_tiles.at[device], tile)[...] * half_mask(half, good)

    load_right = functools.partial(x_tile, lists, own_tiles, other_tiles)
    add_products(lists, groups, load_left, load_right, sums, chunks)

    def store(n, carry):
        square = pair_up(sums[2 * n], sums[2 * n + 1]).astype(jnp.bfloat16)
        for copy in range(out_ref.shape[0]):
            squares[n] = square
        return carry

    lax.fori_loop(0, squares.shape[0], store, 0, unroll=2)
    copies = [
        pltpu.make_async_copy(squares, out_ref.at[n], sent.at[n]) for n in range(out_ref.shape[0])
    ]
    for copy in copies:
        copy.start()
    for copy in copies:
        copy.wait()


def pack_kernel(info, loads, lists, near, sent_ref, out_ref, sent):
    out_ref[...] = jnp.zeros_like(out_ref)
    first, own = info[0], info[1]
    places = (out_ref.shape[1] - META) // 32
    most = jnp.int32(0)
    for target in range(out_ref.shape[0]):
        most = jnp.maximum(most, jnp.where(own == target, 0, loads[0, target]))

    def per_target(target, carry):
        out_ref[target, places * 32 :, :] = jnp.broadcast_to(flat(most), (META, LANES))
        number = jnp.where(target == own, 0, loads[0, target]) - first
        number = jnp.clip(number, 0, places)

        def per_step(step, carry):
            packed = []
            for n in range(STEP):
                both = []
                for half in range(2):
                    place = step * (2 * STEP) + 2 * n + half
                    good = (place < number).astype(jnp.int32)
                    entry = lists[target, jnp.minimum(first + place, lists.shape[1] - 1)]
                    device, tile, side = tile_of(entry, ZSTEP)
                    both.append(to_half(near[device, tile], side, half) * half_mask(half, good))
                packed.append(both[0] + both[1])
            for n, tile in enumerate(packed):
                rows_of(out_ref.at[target], step * STEP + n)[...] = tile
            return carry

        lax.fori_loop(0, lax.div(number + 2 * STEP - 1, 2 * STEP), per_step, 0)
        copy_out(target).start()
        return carry

    def copy_out(target):
        return pltpu.make_async_copy(out_ref.at[target], sent_ref.at[target], sent.at[target])

    def finish(target, carry):
        copy_out(target).wait()
        return carry

    for target in range(out_ref.shape[0]):
        per_target(target, 0)
    lax.fori_loop(0, out_ref.shape[0], finish, 0)


def subtract_cubes(sums, base, out_ref):
    for n in range(out_ref.shape[1] // LANES):
        here = slice(n * LANES, (n + 1) * LANES)
        out_ref[:, here] = base[:, here] - 0.5 * pair_up(sums[2 * n], sums[2 * n + 1])


def near_kernel(
    lists, far, near, own_tiles, other_tiles, base, out_ref, rights, ahead, sums, chunks
):
    def load_left(entry, good):
        device, tile, half = tile_of(entry, ZSTEP)
        return near[device, tile] * half_mask(half, good)

    load_right = functools.partial(x_tile, lists, own_tiles, other_tiles)
    add_products(lists, list_chunks(lists, XROWS, chunks), load_left, load_right, sums, chunks)
    subtract_cubes(sums, base, out_ref)
    ahead[ahead.shape[0] - 1] = list_chunks(far, XROWS, ahead)

    def ready(row, carry):
        for place in range(NEIGH):
            rights[row, place] = x_tile(far, own_tiles, other_tiles, row, place)
        return carry

    lax.fori_loop(0, XROWS, ready, 0)


def largest(far, most_ref):
    places = (far.shape[1] - META) // 32
    most = far[0, places * 32 :, :]
    for n in range(1, far.shape[0]):
        most = jnp.maximum(most, far[n, places * 32 :, :])
    most_ref[0] = jnp.max(most.astype(jnp.float32)).astype(jnp.int32)


def far_tile(far, first, code, good):
    places = (far.shape[1] - META) // 32
    shift = far.shape[0].bit_length() - 1
    group, place = code & (far.shape[0] - 1), (code >> shift) - first
    good = good * ((place >= 0) & (place < places)).astype(jnp.int32)
    place = jnp.clip(place, 0, places - 1)
    return rows_of(far.at[group], place >> 1)[...] * half_mask(place & 1, good)


def first_kernel(lists, ahead, base_hbm, far, rights, out_ref, most_ref, sums, base, arrived):
    fetch = pltpu.make_async_copy(base_hbm, base, arrived)
    fetch.start()
    largest(far, most_ref)
    groups = ahead[ahead.shape[0] - 1]
    load_left = functools.partial(far_tile, far, 0)
    add_products(lists, groups, load_left, lambda row, place: rights[row, place], sums, ahead)
    fetch.wait()
    subtract_cubes(sums, base, out_ref)


def more_kernel(
    info, lists, far, own_tiles, other_tiles, base, out_ref, most_ref, sums, chunks
):
    largest(far, most_ref)
    load_left = functools.partial(far_tile, far, info[0])
    load_right = functools.partial(x_tile, lists, own_tiles, other_tiles)
    add_products(lists, list_chunks(lists, XROWS, chunks), load_left, load_right, sums, chunks)
    subtract_cubes(sums, base, out_ref)


def call(kernel, scalars, arrays, out, scratch=(), far_off=0, out_spec=VMEM):
    single = isinstance(out, jax.ShapeDtypeStruct)
    return pl.pallas_call(
        kernel,
        out_shape=out,
        in_specs=[SMEM] * len(scalars)
        + [pl.BlockSpec(memory_space=pl.ANY)] * far_off
        + [VMEM] * (len(arrays) - far_off),
        out_specs=out_spec if single else [SMEM if len(o.shape) == 1 else VMEM for o in out],
        scratch_shapes=scratch,
        compiler_params=pltpu.CompilerParams(vmem_limit_bytes=20 * MIB),
    )(*scalars, *arrays)


def sums_scratch(rows):
    return [
        pltpu.VMEM((rows, 64, LANES), jnp.float32),
        pltpu.SMEM((rows * 4 + 2 * GROUP,), jnp.int32),
    ]


def numbers(found, n_row, row, n_col, col):
    lines = jnp.stack([found[0] * n_row + row, found[1] * n_col + col])
    return jnp.where(found[0] >= 0, lines, -1.0)


def listed(rows, cols, length):
    lines = jnp.stack([rows, cols])
    return jnp.pad(lines, ((0, 0), (0, length - rows.shape[0])), constant_values=-1)


def sublanes(pairs):
    return jnp.broadcast_to(pairs[:, :, None], (*pairs.shape, LANES))


def send_all(array, axis, count, **groups):
    copies = jnp.broadcast_to(array, (count, *array.shape))
    return lax.all_to_all(copies, axis, split_axis=0, concat_axis=0, **groups)


def per_device(x_values, x_rows, x_cols, z_rows, z_cols):
    x_rows, x_cols, z_rows, z_cols = (a[0, 0] for a in (x_rows, x_cols, z_rows, z_cols))
    own = x_values[0, 0]
    size, width = own.shape
    n_row, n_col = lax.axis_size("row"), lax.axis_size("col")
    n_far = n_col // NEAR
    col = lax.axis_index("col")
    far_own, near_own = col // NEAR, col % NEAR
    near_groups = [[y * NEAR + x for x in range(NEAR)] for y in range(n_far)]
    far_groups = [[y * NEAR + x for y in range(n_far)] for x in range(NEAR)]
    core_groups = [[z + core for z in range(0, n_row, CORES)] for core in range(CORES)]

    row = lax.axis_index("row")

    tiles = own.reshape(size, width // LANES, LANES).transpose(1, 0, 2).reshape(-1, LANES)
    near_tiles = send_all(tiles, "col", NEAR, axis_index_groups=near_groups)
    row_tiles = lax.all_gather(near_tiles, "col", axis=0, axis_index_groups=far_groups)
    row_tiles = row_tiles.reshape(n_col, -1, LANES)

    own_x, own_z = listed(x_rows, x_cols, XROWS), listed(z_rows, z_cols, ZROWS)
    codes = jnp.concatenate([own_x, own_z], axis=1)
    codes = jnp.where(codes[0] >= 0, codes[0] * CODE + codes[1], -1)
    codes = jnp.pad(codes, (0, LANES - codes.shape[0]), constant_values=-1)
    codes, near_tiles = lax.optimization_barrier((codes, near_tiles))
    codes = send_all(codes[None], "col", n_col)[:, 0]
    lines = jnp.where(codes >= 0, jnp.stack([codes // CODE, codes % CODE]), -1)
    row_x = lines[:, :, :XROWS].reshape(2, -1).astype(jnp.float32)
    row_z = lines[:, :, XROWS : XROWS + ZROWS].astype(jnp.float32)

    meta = jnp.stack([codes // CODE // n_row, codes % CODE // n_col])
    meta = jnp.where(codes >= 0, meta, -1)[:, :, :XROWS].astype(own.dtype).reshape(-1, LANES)
    meta = jnp.pad(meta, ((0, META - meta.shape[0]), (0, 0)))
    labelled = jnp.concatenate([tiles, meta])
    own_tiles = send_all(labelled, "row", n_row // CORES, axis_index_groups=core_groups)
    own_z = jnp.pad(own_z, ((0, 0), (0, LANES - ZROWS)), constant_values=-1).astype(jnp.float32)
    own_tiles, row_x, own_z = lax.optimization_barrier((own_tiles, row_x, own_z))
    other_tiles = lax.ppermute(own_tiles, "row", [(n, n ^ 1) for n in range(n_row)])
    core = row % CORES
    devices = jnp.arange(n_col, dtype=jnp.float32)[:, None]
    rows = jnp.arange(n_row // CORES) * CORES
    rows = jnp.stack([rows + core, rows + 1 - core]).astype(jnp.float32)[:, :, None]
    n_lines = 2 * n_col * XROWS // LANES

    def listed_there(t):
        found = t[:, -META : n_lines - META].astype(jnp.float32)
        return found.reshape(n_row // CORES, 2, n_col, XROWS).transpose(1, 0, 2, 3)

    def in_own_col(found, rows):
        found = lax.dynamic_index_in_dim(found, col, 2, keepdims=False)
        return numbers(found, n_row, rows, n_col, col).reshape(2, -1)

    own_listed = listed_there(own_tiles)
    own_col = in_own_col(own_listed, rows[0])
    other_tiles, own_col = lax.optimization_barrier((other_tiles, own_col))
    other_listed = listed_there(other_tiles)
    col_x = (own_col, in_own_col(other_listed, rows[1]))
    all_x = jnp.stack([own_listed, other_listed], axis=1)

    def table(rows):
        return jax.ShapeDtypeStruct((rows, LANES), jnp.int32)


    start = far_own * NEAR % n_row // CORES
    cross = lax.dynamic_slice_in_dim(all_x, start, NEAR // CORES, 2)
    rows = lax.dynamic_slice_in_dim(rows, start, NEAR // CORES, 1)
    in_order = core == 0
    cross = jnp.where(in_order, cross, cross[:, ::-1]).transpose(0, 2, 1, 3, 4)
    rows = jnp.where(in_order, rows, rows[::-1]).transpose(1, 0, 2).reshape(NEAR, 1, 1)
    cross = cross.reshape(2, NEAR, n_col, XROWS)
    cross = numbers(cross, n_row, rows, n_col, devices)
    targets = jnp.arange(n_col)[:, None]
    cross_k = jnp.where(targets % NEAR == near_own, cross[0], -1.0)
    cross_y = jnp.broadcast_to((targets // NEAR).astype(jnp.float32), cross_k.shape)
    cross_x = jnp.stack([cross_k, cross[1], cross_y], axis=1).reshape(NEAR, 3, -1)
    near_z = lax.dynamic_slice_in_dim(row_z, far_own * NEAR, NEAR, 1).reshape(2, -1)
    row_z = jnp.pad(row_z, ((0, 0), (0, 0), (0, ZSTEP - ZROWS)), constant_values=-1)
    own_x = sublanes(own_x.astype(jnp.float32))
    near_list, far_list = call(
        cube_match,
        (far_own.reshape(1),),
        (own_x, row_z.reshape(2, -1), *col_x),
        (table(XROWS), table(XROWS)),
    )
    send_list, loads = call(
        send_kernel,
        (),
        (sublanes(near_z), row_x, cross_x),
        (jax.ShapeDtypeStruct((n_far, SEGMENT), jnp.int32), table(1)),
        [pltpu.VMEM((SEGMENT, LANES), jnp.float32)],
    )
    square = call(
        square_kernel,
        (),
        (
            pltpu.with_memory_space_constraint(row_tiles, pltpu.HBM),
            own_z,
            row_x,
            *col_x,
            own_tiles,
            other_tiles,
        ),
        jax.ShapeDtypeStruct((NEAR, z_rows.shape[0] // 2, size, LANES), jnp.bfloat16),
        [
            *sums_scratch(ZROWS),
            pltpu.VMEM(row_tiles.shape, row_tiles.dtype),
            pltpu.SemaphoreType.DMA((4,)),
            pltpu.VMEM((ZROWS, LANES), jnp.int32),
            pltpu.SMEM((ZROWS, LANES), jnp.int32),
            pltpu.SemaphoreType.DMA,
            pltpu.VMEM((z_rows.shape[0] // 2, size, LANES), jnp.bfloat16),
            pltpu.SemaphoreType.DMA((NEAR,)),
        ],
        far_off=1,
        out_spec=pl.BlockSpec(memory_space=pl.ANY),
    )
    near = lax.all_to_all(
        square, "col", split_axis=0, concat_axis=0, axis_index_groups=near_groups
    )

    def exchange(first, count):
        info = jnp.stack([first, far_own])
        packed = call(
            pack_kernel,
            (info, loads, send_list),
            (near,),
            jax.ShapeDtypeStruct((n_far, count * size + META, LANES), jnp.bfloat16),
            [
                pltpu.VMEM((n_far, count * size + META, LANES), jnp.bfloat16),
                pltpu.SemaphoreType.DMA((n_far,)),
            ],
            out_spec=pl.BlockSpec(memory_space=pl.ANY),
        )
        far = lax.all_to_all(
            packed, "col", split_axis=0, concat_axis=0, axis_index_groups=far_groups
        )
        return info, far

    used = jnp.repeat((x_rows >= 0).astype(jnp.float32), size)
    base = 1.5 * own.astype(jnp.float32) * used[None]
    ahead = jax.ShapeDtypeStruct((XROWS * 4 + 2 * GROUP,), jnp.int32)
    result, most = jax.ShapeDtypeStruct(base.shape, jnp.float32), jax.ShapeDtypeStruct((1,), jnp.int32)
    rights = pltpu.VMEM((XROWS, NEIGH, size, LANES), own.dtype)
    base, rights, ahead = call(
        near_kernel,
        (near_list, far_list),
        (near, own_tiles, other_tiles, base),
        (result, rights, ahead),
        sums_scratch(XROWS),
    )
    _, far = exchange(jnp.int32(0), FIRST)
    state = call(
        first_kernel,
        (far_list, ahead),
        (pltpu.with_memory_space_constraint(base, pltpu.HBM), far, rights),
        (result, most),
        [
            sums_scratch(XROWS)[0],
            pltpu.VMEM(base.shape, jnp.float32),
            pltpu.SemaphoreType.DMA,
        ],
        far_off=1,
    )

    def more(state):
        first, base, _ = state
        info, far = exchange(first, MORE)
        base, largest_need = call(
            more_kernel,
            (info, far_list),
            (far, own_tiles, other_tiles, base),
            (result, most),
            sums_scratch(XROWS),
        )
        return first + 2 * MORE, base, largest_need

    state = (jnp.int32(2 * FIRST), *state)
    _, result, _ = lax.while_loop(lambda state: state[0] < state[2][0], more, state)
    return result[None, None]


def solution(mesh):
    placed = (
        P("row", "col", None, None),
        P("row", "col", None),
        P("row", "col", None),
        P("row", "col", None),
        P("row", "col", None),
    )
    return jax.shard_map(
        per_device,
        mesh=mesh,
        in_specs=placed,
        out_specs=P("row", "col", None, None),
        check_vma=False,
    )
```

```python
import functools

import jax
import jax.numpy as jnp
from jax import lax
from jax.experimental import pallas as pl
from jax.experimental.pallas import tpu as pltpu
from jax.sharding import PartitionSpec as P

NEIGH = 7
CODE = 512
CORES = 2
NEAR = 4
XROWS = 16
ZROWS = 40
ZSTEP = 64
SEGMENT = NEAR * ZSTEP
FIRST = 12
MORE = 2
META = 16
LANES = 128
CHUNK = 2
GROUP = 16
STEP = 2
COUNT = 32
FAR = 1e9
MIB = 1024 * 1024
VMEM = pl.BlockSpec(memory_space=pltpu.VMEM)
SMEM = pl.BlockSpec(memory_space=pltpu.SMEM)


def lane_numbers(width):
    return lax.broadcasted_iota(jnp.int32, (1, width), 1).astype(jnp.float32)


def upright(row):
    return jnp.broadcast_to(row, (LANES, LANES)).T


def beside(*refs):
    return (jnp.concatenate([ref[n : n + 1, :] for ref in refs], axis=1) for n in range(2))


def following(hits, lanes, last):
    return jnp.min(jnp.where(hits & (lanes > last), lanes, FAR), axis=1, keepdims=True)


def picked(hits, values):
    return jnp.sum(jnp.where(hits, values, 0.0), axis=1, keepdims=True)


def put(table, base, count, good, value):
    return jnp.where((lane_numbers(LANES) == base + count) & good, value, table)


def square_match(own_z, row_x, own_col, other_col):
    row_i, row_m = row_x[0:1, :], row_x[1:2, :]
    col_m, col_k = beside(own_col, other_col)
    row_lanes, col_lanes = lane_numbers(row_i.shape[1]), lane_numbers(col_m.shape[1])
    lane = lane_numbers(LANES)

    i, k = (upright(own_z[n : n + 1, :])[:ZROWS, :1] for n in range(2))
    in_row, in_col = (row_i == i) & (i >= 0), (col_k == k) & (k >= 0)
    table = jnp.zeros((ZROWS, LANES), jnp.float32)
    count = jnp.zeros((ZROWS, 1), jnp.float32)
    last = count - 1
    for _ in range(NEIGH):
        last = following(in_row, row_lanes, last)
        middle = picked(row_lanes == last, row_m)
        found = picked(in_col & (col_m == middle), col_lanes + 1)
        good = (last < FAR) & (found > 0)
        table = put(table, 0, count, good, last)
        table = put(table, 8, count, good, found - 1)
        count = count + jnp.where(good, 1.0, 0.0)
    return jnp.where(lane == COUNT, count, table).astype(jnp.int32)

def cube_match(here, own_x, row_z, own_col, other_col, near_list, far_list):
    col_m, col_k = beside(own_col, other_col)
    col_lanes, lane = lane_numbers(col_m.shape[1]), lane_numbers(LANES)
    z_lanes = lane_numbers(row_z.shape[1])
    z_i, z_k = row_z[0:1, :], row_z[1:2, :]
    i, j = own_x[0][:, :1], own_x[1][:, :1]
    in_col = (col_k == j) & (j >= 0)
    needed = jnp.zeros((1, row_z.shape[1]), jnp.float32)
    entries = []
    last = jnp.full((XROWS, 1), -1.0, jnp.float32)
    for _ in range(NEIGH):
        last = following(in_col, col_lanes, last)
        middle = picked(col_lanes == last, col_m)
        hits = (z_i == i) & (z_k == middle) & (last < FAR)
        needed = jnp.maximum(
            needed, jnp.max(jnp.where(hits, 1.0, 0.0), axis=0, keepdims=True)
        )
        entries.append((last, picked(hits, z_lanes + 1) - 1))
    needed = jnp.concatenate(
        [needed[:, n : n + SEGMENT] for n in range(0, needed.shape[1], SEGMENT)], axis=0
    )
    before = (
        lax.broadcasted_iota(jnp.int32, (SEGMENT, SEGMENT), 0)
        < lax.broadcasted_iota(jnp.int32, (SEGMENT, SEGMENT), 1)
    ).astype(jnp.float32)
    rank = jnp.dot(needed, before, preferred_element_type=jnp.float32)
    n_groups = rank.shape[0]
    rank = jnp.concatenate([rank[n : n + 1] for n in range(rank.shape[0])], axis=1)
    own = here[0].astype(jnp.float32)
    for near, out_ref in ((True, near_list), (False, far_list)):
        table = jnp.zeros((XROWS, LANES), jnp.float32)
        count = jnp.zeros((XROWS, 1), jnp.float32)
        for last, entry in entries:
            group = jnp.floor(entry / SEGMENT)
            entry_of = entry - group * SEGMENT
            if near:
                good = (entry >= 0) & (group == own)
                value = entry_of
            else:
                good = (entry >= 0) & (group != own)
                value = picked(z_lanes == entry, rank) * n_groups + group
            table = put(table, 0, count, good, value)
            table = put(table, 8, count, good, last)
            count = count + jnp.where(good, 1.0, 0.0)
        out_ref[...] = jnp.where(lane == COUNT, count, table).astype(jnp.int32)


def send_kernel(near_z, row_x, cross_x, send_list, loads, ranked):
    row_i, row_m = row_x[0:1, :], row_x[1:2, :]
    row_lanes, lane = lane_numbers(row_i.shape[1]), lane_numbers(LANES)
    needs, numbers = [], []
    for n in range(NEAR):
        here = slice(n * ZROWS, (n + 1) * ZROWS)
        i, k = near_z[0][here, :1], near_z[1][here, :1]
        cross_k, cross_j, cross_y = (cross_x[n][t : t + 1, :] for t in range(3))
        in_row, in_cross = (row_i == i) & (i >= 0), (cross_k == k) & (k >= 0)
        need = jnp.zeros((ZROWS, LANES), jnp.float32)
        last = jnp.full((ZROWS, 1), -1.0, jnp.float32)
        for _ in range(NEIGH):
            last = following(in_cross, row_lanes, last)
            target = picked(row_lanes == last, cross_j)
            far = picked(row_lanes == last, cross_y)
            found = picked(in_row & (row_m == target), 1.0)
            need = jnp.where((lane == far) & (last < FAR) & (found > 0), 1.0, need)
        needs.append(need)
        numbers.append(lax.broadcasted_iota(jnp.int32, need.shape, 0) + n * ZSTEP)
    need = jnp.concatenate(needs, axis=0)
    number = jnp.concatenate(numbers, axis=0).astype(jnp.float32)
    size = need.shape[0]
    before = (
        lax.broadcasted_iota(jnp.int32, (size, size), 1)
        < lax.broadcasted_iota(jnp.int32, (size, size), 0)
    ).astype(jnp.float32)
    rank = jnp.dot(before, need, preferred_element_type=jnp.float32)
    rank = jnp.where(need > 0, rank, -1.0)

    def list_rank(p, carry):
        at = rank == p.astype(jnp.float32)
        row = jnp.sum(jnp.where(at, number, 0.0), axis=0, keepdims=True)
        ranked[pl.ds(p, 1), :] = row
        return carry

    ranked[...] = jnp.zeros_like(ranked)
    lax.fori_loop(0, size, list_rank, 0)
    send_list[...] = ranked[...].T[: send_list.shape[0], :].astype(jnp.int32)
    loads[...] = jnp.sum(need, axis=0, keepdims=True).astype(jnp.int32)


def half_mask(half, good):
    lane = lax.broadcasted_iota(jnp.int32, (1, LANES), 1)
    kept = jnp.where(good > 0, half, 2)
    return jnp.where(lane >> 6 == kept, 1.0, 0.0).astype(jnp.bfloat16)


def flat(value):
    return jnp.full((1, LANES), value.astype(jnp.float32)).astype(jnp.bfloat16)


def to_half(tile, half, want):
    swapped = jnp.concatenate([tile[:, 64:], tile[:, :64]], axis=1)
    other = (half != want).astype(jnp.int32)
    return tile * flat(1 - other) + swapped * flat(other)


def pair_up(even, odd):
    even, odd = (tile + pltpu.roll(tile, 64, 1) for tile in (even, odd))
    lane = lax.broadcasted_iota(jnp.int32, even.shape, 1)
    return jnp.where(lane < 64, even, odd)


def list_chunks(lists, rows, chunks):
    length = jnp.int32(0)
    for n in range(rows - 1):
        for start in range(0, NEIGH, CHUNK):
            chunks[length + start // CHUNK] = (n << 3) + start
        length = length + lax.div(lists[n, COUNT] + CHUNK - 1, CHUNK)
    for spare in range(GROUP):
        chunks[length + spare] = (rows - 1) << 3
    return lax.div(length + GROUP - 1, GROUP)


def add_products(lists, groups, load_left, load_right, sums, chunks):
    sums[...] = jnp.zeros_like(sums)

    def per_group(group, carry):
        values = []
        for n in range(GROUP):
            code = chunks[group * GROUP + n]
            row, start = code >> 3, code & 7
            left, right = [], []
            for t in range(CHUNK):
                place = jnp.minimum(start + t, NEIGH - 1)
                good = (start + t < lists[row, COUNT]).astype(jnp.int32)
                left.append(load_left(lists[row, place], good))
                tile = load_right(row, place)
                right += [tile, tile]
            left, right = jnp.concatenate(left, axis=1), jnp.concatenate(right, axis=0)
            values.append((row, jnp.dot(left, right, preferred_element_type=jnp.float32)))
        for row, value in values:
            sums[row] += value
        return carry

    lax.fori_loop(0, groups, per_group, 0)


def tile_of(entry, step):
    shift = step.bit_length() - 1
    return entry >> shift, (entry & (step - 1)) >> 1, entry & 1


def rows_of(ref, tile):
    return ref.at[pl.ds(pl.multiple_of(tile * 64, 64), 64), :]


def x_tile(lists, own, other, row, place):
    device, tile, half = tile_of(lists[row, 8 + place], XROWS)
    shift = own.shape[0].bit_length() - 1
    core, device = device >> shift, device & (own.shape[0] - 1)
    tiles = (rows_of(ref.at[device], tile)[...] for ref in (own, other))
    own_tile, other_tile = tiles
    return own_tile * half_mask(half, 1 - core) + other_tile * half_mask(half, core)


def square_kernel(
    row_hbm, own_z, row_x, own_col, other_col, own_tiles, other_tiles, out_ref, *scratch
):
    sums, chunks, row_tiles, arrived, table, lists, listed, squares, sent = scratch
    parts = arrived.shape[0]
    step = row_tiles.shape[0] // parts
    fetches = [
        pltpu.make_async_copy(
            row_hbm.at[pl.ds(n * step, step)], row_tiles.at[pl.ds(n * step, step)], arrived.at[n]
        )
        for n in range(parts)
    ]
    for fetch in fetches:
        fetch.start()
    table[...] = square_match(own_z, row_x, own_col, other_col)
    known = pltpu.make_async_copy(table, lists, listed)
    known.start()
    known.wait()
    groups = list_chunks(lists, ZROWS, chunks)
    for fetch in fetches:
        fetch.wait()

    def load_left(entry, good):
        device, tile, half = tile_of(entry, XROWS)
        return rows_of(row_tiles.at[device], tile)[...] * half_mask(half, good)

    load_right = functools.partial(x_tile, lists, own_tiles, other_tiles)
    add_products(lists, groups, load_left, load_right, sums, chunks)

    def store(n, carry):
        square = pair_up(sums[2 * n], sums[2 * n + 1]).astype(jnp.bfloat16)
        for copy in range(out_ref.shape[0]):
            squares[n] = square
        return carry

    lax.fori_loop(0, squares.shape[0], store, 0, unroll=6)
    copies = [
        pltpu.make_async_copy(squares, out_ref.at[n], sent.at[n]) for n in range(out_ref.shape[0])
    ]
    for copy in copies:
        copy.start()
    for copy in copies:
        copy.wait()


def pack_kernel(info, loads, lists, near, sent_ref, out_ref, sent):
    out_ref[...] = jnp.zeros_like(out_ref)
    first, own = info[0], info[1]
    places = (out_ref.shape[1] - META) // 32
    most = jnp.int32(0)
    for target in range(out_ref.shape[0]):
        most = jnp.maximum(most, jnp.where(own == target, 0, loads[0, target]))

    def per_target(target, carry):
        out_ref[target, places * 32 :, :] = jnp.broadcast_to(flat(most), (META, LANES))
        number = jnp.where(target == own, 0, loads[0, target]) - first
        number = jnp.clip(number, 0, places)

        def per_step(step, carry):
            packed = []
            for n in range(STEP):
                both = []
                for half in range(2):
                    place = step * (2 * STEP) + 2 * n + half
                    good = (place < number).astype(jnp.int32)
                    entry = lists[target, jnp.minimum(first + place, lists.shape[1] - 1)]
                    device, tile, side = tile_of(entry, ZSTEP)
                    both.append(to_half(near[device, tile], side, half) * half_mask(half, good))
                packed.append(both[0] + both[1])
            for n, tile in enumerate(packed):
                rows_of(out_ref.at[target], step * STEP + n)[...] = tile
            return carry

        lax.fori_loop(0, lax.div(number + 2 * STEP - 1, 2 * STEP), per_step, 0)
        copy_out(target).start()
        return carry

    def copy_out(target):
        return pltpu.make_async_copy(out_ref.at[target], sent_ref.at[target], sent.at[target])

    def finish(target, carry):
        copy_out(target).wait()
        return carry

    for target in range(out_ref.shape[0]):
        per_target(target, 0)
    lax.fori_loop(0, out_ref.shape[0], finish, 0)


def subtract_cubes(sums, base, out_ref):
    for n in range(out_ref.shape[1] // LANES):
        here = slice(n * LANES, (n + 1) * LANES)
        out_ref[:, here] = base[:, here] - 0.5 * pair_up(sums[2 * n], sums[2 * n + 1])


def near_kernel(
    lists, far, near, own_tiles, other_tiles, base, out_ref, rights, ahead, sums, chunks
):
    def load_left(entry, good):
        device, tile, half = tile_of(entry, ZSTEP)
        return near[device, tile] * half_mask(half, good)

    load_right = functools.partial(x_tile, lists, own_tiles, other_tiles)
    add_products(lists, list_chunks(lists, XROWS, chunks), load_left, load_right, sums, chunks)
    subtract_cubes(sums, base, out_ref)
    ahead[ahead.shape[0] - 1] = list_chunks(far, XROWS, ahead)

    def ready(row, carry):
        for place in range(NEIGH):
            rights[row, place] = x_tile(far, own_tiles, other_tiles, row, place)
        return carry

    lax.fori_loop(0, XROWS, ready, 0)


def largest(far, most_ref):
    places = (far.shape[1] - META) // 32
    most = far[0, places * 32 :, :]
    for n in range(1, far.shape[0]):
        most = jnp.maximum(most, far[n, places * 32 :, :])
    most_ref[0] = jnp.max(most.astype(jnp.float32)).astype(jnp.int32)


def far_tile(far, first, code, good):
    places = (far.shape[1] - META) // 32
    shift = far.shape[0].bit_length() - 1
    group, place = code & (far.shape[0] - 1), (code >> shift) - first
    good = good * ((place >= 0) & (place < places)).astype(jnp.int32)
    place = jnp.clip(place, 0, places - 1)
    return rows_of(far.at[group], place >> 1)[...] * half_mask(place & 1, good)


def first_kernel(lists, ahead, base_hbm, far, rights, out_ref, most_ref, sums, base, arrived):
    fetch = pltpu.make_async_copy(base_hbm, base, arrived)
    fetch.start()
    largest(far, most_ref)
    groups = ahead[ahead.shape[0] - 1]
    load_left = functools.partial(far_tile, far, 0)
    add_products(lists, groups, load_left, lambda row, place: rights[row, place], sums, ahead)
    fetch.wait()
    subtract_cubes(sums, base, out_ref)


def more_kernel(
    info, lists, far, own_tiles, other_tiles, base, out_ref, most_ref, sums, chunks
):
    largest(far, most_ref)
    load_left = functools.partial(far_tile, far, info[0])
    load_right = functools.partial(x_tile, lists, own_tiles, other_tiles)
    add_products(lists, list_chunks(lists, XROWS, chunks), load_left, load_right, sums, chunks)
    subtract_cubes(sums, base, out_ref)


def call(kernel, scalars, arrays, out, scratch=(), far_off=0, out_spec=VMEM):
    single = isinstance(out, jax.ShapeDtypeStruct)
    return pl.pallas_call(
        kernel,
        out_shape=out,
        in_specs=[SMEM] * len(scalars)
        + [pl.BlockSpec(memory_space=pl.ANY)] * far_off
        + [VMEM] * (len(arrays) - far_off),
        out_specs=out_spec if single else [SMEM if len(o.shape) == 1 else VMEM for o in out],
        scratch_shapes=scratch,
        compiler_params=pltpu.CompilerParams(vmem_limit_bytes=20 * MIB),
    )(*scalars, *arrays)


def sums_scratch(rows):
    return [
        pltpu.VMEM((rows, 64, LANES), jnp.float32),
        pltpu.SMEM((rows * 4 + 2 * GROUP,), jnp.int32),
    ]


def numbers(found, n_row, row, n_col, col):
    lines = jnp.stack([found[0] * n_row + row, found[1] * n_col + col])
    return jnp.where(found[0] >= 0, lines, -1.0)


def listed(rows, cols, length):
    lines = jnp.stack([rows, cols])
    return jnp.pad(lines, ((0, 0), (0, length - rows.shape[0])), constant_values=-1)


def sublanes(pairs):
    return jnp.broadcast_to(pairs[:, :, None], (*pairs.shape, LANES))


def send_all(array, axis, count, **groups):
    copies = jnp.broadcast_to(array, (count, *array.shape))
    return lax.all_to_all(copies, axis, split_axis=0, concat_axis=0, **groups)


def per_device(x_values, x_rows, x_cols, z_rows, z_cols):
    x_rows, x_cols, z_rows, z_cols = (a[0, 0] for a in (x_rows, x_cols, z_rows, z_cols))
    own = x_values[0, 0]
    size, width = own.shape
    n_row, n_col = lax.axis_size("row"), lax.axis_size("col")
    n_far = n_col // NEAR
    col = lax.axis_index("col")
    far_own, near_own = col // NEAR, col % NEAR
    near_groups = [[y * NEAR + x for x in range(NEAR)] for y in range(n_far)]
    far_groups = [[y * NEAR + x for y in range(n_far)] for x in range(NEAR)]
    core_groups = [[z + core for z in range(0, n_row, CORES)] for core in range(CORES)]

    row = lax.axis_index("row")

    tiles = own.reshape(size, width // LANES, LANES).transpose(1, 0, 2).reshape(-1, LANES)
    near_tiles = send_all(tiles, "col", NEAR, axis_index_groups=near_groups)
    row_tiles = lax.all_gather(near_tiles, "col", axis=0, axis_index_groups=far_groups)
    row_tiles = row_tiles.reshape(n_col, -1, LANES)

    own_x, own_z = listed(x_rows, x_cols, XROWS), listed(z_rows, z_cols, ZROWS)
    codes = jnp.concatenate([own_x, own_z], axis=1)
    codes = jnp.where(codes[0] >= 0, codes[0] * CODE + codes[1], -1)
    codes = jnp.pad(codes, (0, LANES - codes.shape[0]), constant_values=-1)
    codes, near_tiles = lax.optimization_barrier((codes, near_tiles))
    codes = send_all(codes[None], "col", n_col)[:, 0]
    lines = jnp.where(codes >= 0, jnp.stack([codes // CODE, codes % CODE]), -1)
    row_x = lines[:, :, :XROWS].reshape(2, -1).astype(jnp.float32)
    row_z = lines[:, :, XROWS : XROWS + ZROWS].astype(jnp.float32)

    meta = jnp.stack([codes // CODE // n_row, codes % CODE // n_col])
    meta = jnp.where(codes >= 0, meta, -1)[:, :, :XROWS].astype(own.dtype).reshape(-1, LANES)
    meta = jnp.pad(meta, ((0, META - meta.shape[0]), (0, 0)))
    labelled = jnp.concatenate([tiles, meta])
    own_tiles = send_all(labelled, "row", n_row // CORES, axis_index_groups=core_groups)
    own_z = jnp.pad(own_z, ((0, 0), (0, LANES - ZROWS)), constant_values=-1).astype(jnp.float32)
    own_tiles, row_x, own_z = lax.optimization_barrier((own_tiles, row_x, own_z))
    other_tiles = lax.ppermute(own_tiles, "row", [(n, n ^ 1) for n in range(n_row)])
    core = row % CORES
    devices = jnp.arange(n_col, dtype=jnp.float32)[:, None]
    rows = jnp.arange(n_row // CORES) * CORES
    rows = jnp.stack([rows + core, rows + 1 - core]).astype(jnp.float32)[:, :, None]
    n_lines = 2 * n_col * XROWS // LANES

    def listed_there(t):
        found = t[:, -META : n_lines - META].astype(jnp.float32)
        return found.reshape(n_row // CORES, 2, n_col, XROWS).transpose(1, 0, 2, 3)

    def in_own_col(found, rows):
        found = lax.dynamic_index_in_dim(found, col, 2, keepdims=False)
        return numbers(found, n_row, rows, n_col, col).reshape(2, -1)

    own_listed = listed_there(own_tiles)
    own_col = in_own_col(own_listed, rows[0])
    other_tiles, own_col = lax.optimization_barrier((other_tiles, own_col))
    other_listed = listed_there(other_tiles)
    col_x = (own_col, in_own_col(other_listed, rows[1]))
    all_x = jnp.stack([own_listed, other_listed], axis=1)

    def table(rows):
        return jax.ShapeDtypeStruct((rows, LANES), jnp.int32)


    start = far_own * NEAR % n_row // CORES
    cross = lax.dynamic_slice_in_dim(all_x, start, NEAR // CORES, 2)
    rows = lax.dynamic_slice_in_dim(rows, start, NEAR // CORES, 1)
    in_order = core == 0
    cross = jnp.where(in_order, cross, cross[:, ::-1]).transpose(0, 2, 1, 3, 4)
    rows = jnp.where(in_order, rows, rows[::-1]).transpose(1, 0, 2).reshape(NEAR, 1, 1)
    cross = cross.reshape(2, NEAR, n_col, XROWS)
    cross = numbers(cross, n_row, rows, n_col, devices)
    targets = jnp.arange(n_col)[:, None]
    cross_k = jnp.where(targets % NEAR == near_own, cross[0], -1.0)
    cross_y = jnp.broadcast_to((targets // NEAR).astype(jnp.float32), cross_k.shape)
    cross_x = jnp.stack([cross_k, cross[1], cross_y], axis=1).reshape(NEAR, 3, -1)
    near_z = lax.dynamic_slice_in_dim(row_z, far_own * NEAR, NEAR, 1).reshape(2, -1)
    row_z = jnp.pad(row_z, ((0, 0), (0, 0), (0, ZSTEP - ZROWS)), constant_values=-1)
    own_x = sublanes(own_x.astype(jnp.float32))
    near_list, far_list = call(
        cube_match,
        (far_own.reshape(1),),
        (own_x, row_z.reshape(2, -1), *col_x),
        (table(XROWS), table(XROWS)),
    )
    send_list, loads = call(
        send_kernel,
        (),
        (sublanes(near_z), row_x, cross_x),
        (jax.ShapeDtypeStruct((n_far, SEGMENT), jnp.int32), table(1)),
        [pltpu.VMEM((SEGMENT, LANES), jnp.float32)],
    )
    square = call(
        square_kernel,
        (),
        (
            pltpu.with_memory_space_constraint(row_tiles, pltpu.HBM),
            own_z,
            row_x,
            *col_x,
            own_tiles,
            other_tiles,
        ),
        jax.ShapeDtypeStruct((NEAR, z_rows.shape[0] // 2, size, LANES), jnp.bfloat16),
        [
            *sums_scratch(ZROWS),
            pltpu.VMEM(row_tiles.shape, row_tiles.dtype),
            pltpu.SemaphoreType.DMA((4,)),
            pltpu.VMEM((ZROWS, LANES), jnp.int32),
            pltpu.SMEM((ZROWS, LANES), jnp.int32),
            pltpu.SemaphoreType.DMA,
            pltpu.VMEM((z_rows.shape[0] // 2, size, LANES), jnp.bfloat16),
            pltpu.SemaphoreType.DMA((NEAR,)),
        ],
        far_off=1,
        out_spec=pl.BlockSpec(memory_space=pl.ANY),
    )
    near = lax.all_to_all(
        square, "col", split_axis=0, concat_axis=0, axis_index_groups=near_groups
    )

    def exchange(first, count):
        info = jnp.stack([first, far_own])
        packed = call(
            pack_kernel,
            (info, loads, send_list),
            (near,),
            jax.ShapeDtypeStruct((n_far, count * size + META, LANES), jnp.bfloat16),
            [
                pltpu.VMEM((n_far, count * size + META, LANES), jnp.bfloat16),
                pltpu.SemaphoreType.DMA((n_far,)),
            ],
            out_spec=pl.BlockSpec(memory_space=pl.ANY),
        )
        far = lax.all_to_all(
            packed, "col", split_axis=0, concat_axis=0, axis_index_groups=far_groups
        )
        return info, far

    used = jnp.repeat((x_rows >= 0).astype(jnp.float32), size)
    base = 1.5 * own.astype(jnp.float32) * used[None]
    ahead = jax.ShapeDtypeStruct((XROWS * 4 + 2 * GROUP,), jnp.int32)
    result, most = jax.ShapeDtypeStruct(base.shape, jnp.float32), jax.ShapeDtypeStruct((1,), jnp.int32)
    rights = pltpu.VMEM((XROWS, NEIGH, size, LANES), own.dtype)
    base, rights, ahead = call(
        near_kernel,
        (near_list, far_list),
        (near, own_tiles, other_tiles, base),
        (result, rights, ahead),
        sums_scratch(XROWS),
    )
    _, far = exchange(jnp.int32(0), FIRST)
    state = call(
        first_kernel,
        (far_list, ahead),
        (pltpu.with_memory_space_constraint(base, pltpu.HBM), far, rights),
        (result, most),
        [
            sums_scratch(XROWS)[0],
            pltpu.VMEM(base.shape, jnp.float32),
            pltpu.SemaphoreType.DMA,
        ],
        far_off=1,
    )

    def more(state):
        first, base, _ = state
        info, far = exchange(first, MORE)
        base, largest_need = call(
            more_kernel,
            (info, far_list),
            (far, own_tiles, other_tiles, base),
            (result, most),
            sums_scratch(XROWS),
        )
        return first + 2 * MORE, base, largest_need

    state = (jnp.int32(2 * FIRST), *state)
    _, result, _ = lax.while_loop(lambda state: state[0] < state[2][0], more, state)
    return result[None, None]


def solution(mesh):
    placed = (
        P("row", "col", None, None),
        P("row", "col", None),
        P("row", "col", None),
        P("row", "col", None),
        P("row", "col", None),
    )
    return jax.shard_map(
        per_device,
        mesh=mesh,
        in_specs=placed,
        out_specs=P("row", "col", None, None),
        check_vma=False,
    )
```
